32 devices in a mesh: ctx: 16 (over z, y, x), head: 2 (over core).
Axes of the slice: x: 2, y: 2, z: 4, core: 2. Of those that a mesh axis runs over, the one named last changes fastest.
Arguments:
- queries: bfloat16 [2, 8192, 2, 512], P(None, 'ctx', 'head'), may hold values from -6 to 6
- key_vectors: bfloat16 [2, 8192, 2, 512], P(None, 'ctx', 'head'), may hold values from -6 to 6
- value_vectors: bfloat16 [2, 8192, 2, 512], P(None, 'ctx', 'head'), may hold values from -6 to 6
- token_rates: float32 [2, 8192, 2], P(None, 'ctx', 'head'), may hold values from 0.02 to 0.5
- fast_init: bfloat16 [2, 3, 512, 512], P('head'), may hold values from -0.25 to 0.25
- out_proj: bfloat16 [2, 512, 2048], P('head'), may hold values from -0.1875 to 0.1875
Outputs:
- layer_out: bfloat16 [2, 8192, 2048], P(None, 'ctx', 'head')
The draws below stay inside these ranges and needn't reach their ends.
All inputs are finite; a program needn't handle non-finite values.
Results may differ from the reference program's by a relative error of at most 0.018.
Values may be sent and summed in bfloat16 or wider, within the bound.
No kernel may reach another device: no remote copies, remote signals or barrier semaphores. Data moves between devices by JAX's collectives and lax.ppermute only.
A program may use at most 128 MiB of HBM per device.

```python
import math
import jax
import jax.numpy as jnp
from jax import lax

D = 2048
HEADS = 2
HD = 512
BLOCKS = 2
CTOK = 8192


def block_scale(key, dims, pieces, low, largest):
    factor_of = 1.0
    for dim, blocks in pieces:
        draws = jax.random.uniform(jax.random.fold_in(jax.random.fold_in(key, 6), dim), (blocks,), jnp.float32, low / len(pieces), largest / len(pieces))
        factor_of = factor_of * jnp.repeat(jnp.exp(draws), dims[dim] // blocks).reshape((-1,) + (1,) * (len(dims) - 1 - dim))
    return factor_of


def bell_draw(rng, dims, spread, reach, cuts=(), dtype=jnp.bfloat16):
    entries = spread * jax.random.normal(rng, dims, jnp.float32)
    if cuts:
        entries = entries * block_scale(rng, dims, cuts, -0.22, 0.18)
    return jnp.clip(entries, -reach, reach).astype(dtype)


def setup_inputs(seed: int = 0) -> dict:
    key_list = jax.random.split(jax.random.key(seed), 7)
    queries = bell_draw(key_list[0], (BLOCKS, CTOK, HEADS, HD), 1.0, 6.0, ((1, 16), (2, 2)))
    key_vectors = bell_draw(key_list[1], (BLOCKS, CTOK, HEADS, HD), 1.0, 6.0, ((1, 16), (2, 2)))
    value_vectors = bell_draw(key_list[2], (BLOCKS, CTOK, HEADS, HD), 1.0, 6.0, ((1, 16), (2, 2)))
    token_rates = jnp.clip(jnp.exp(math.log(0.5) - 3.218876 * jax.random.uniform(key_list[3], (BLOCKS, CTOK, HEADS), jnp.float32) ** block_scale(key_list[3], (BLOCKS, CTOK, HEADS), ((1, 16), (2, 2)), -0.2, 0.2)), 0.02, 0.5)
    fast_init = bell_draw(key_list[4], (HEADS, 3, HD, HD), HD ** -0.5, 0.25, ((0, 2),))
    out_proj = bell_draw(key_list[5], (HEADS, HD, D), (HEADS * HD) ** -0.5, 0.1875, ((0, 2),))
    return dict(queries=queries, key_vectors=key_vectors, value_vectors=value_vectors, token_rates=token_rates, fast_init=fast_init, out_proj=out_proj)


momentum_beta = 0.9
step_size = 0.03

def silu_of(values):
    return values * jax.nn.sigmoid(values)

def fast_grads(weights_bf, key_rows, value_rows, rates):
    gate_pre = jnp.dot(key_rows, weights_bf[0], preferred_element_type=jnp.float32)
    lin_pre = jnp.dot(key_rows, weights_bf[1], preferred_element_type=jnp.float32)
    sig_gate = jax.nn.sigmoid(gate_pre)
    silu_out = gate_pre * sig_gate
    hidden = (silu_out * lin_pre).astype(jnp.bfloat16)
    out_grad = (rates[:, None] * value_rows.astype(jnp.float32)).astype(jnp.bfloat16)
    hid_grad = lax.dot_general(out_grad, weights_bf[2], (((1,), (1,)), ((), ())), preferred_element_type=jnp.float32)
    gate_grad = (hid_grad * lin_pre * sig_gate * (1.0 + gate_pre * (1.0 - sig_gate))).astype(jnp.bfloat16)
    lin_grad = (hid_grad * silu_out).astype(jnp.bfloat16)
    contract = (((0,), (0,)), ((), ()))
    grad_gate = lax.dot_general(key_rows, gate_grad, contract, preferred_element_type=jnp.float32)
    grad_lin = lax.dot_general(key_rows, lin_grad, contract, preferred_element_type=jnp.float32)
    grad_out = lax.dot_general(hidden, out_grad, contract, preferred_element_type=jnp.float32)
    return jnp.stack([grad_gate, grad_lin, grad_out])

def fast_apply(weights_bf, query_rows):
    gate_pre = jnp.dot(query_rows, weights_bf[0], preferred_element_type=jnp.float32)
    lin_pre = jnp.dot(query_rows, weights_bf[1], preferred_element_type=jnp.float32)
    hidden = (silu_of(gate_pre) * lin_pre).astype(jnp.bfloat16)
    return jnp.dot(hidden, weights_bf[2], preferred_element_type=jnp.float32).astype(jnp.bfloat16)

def renorm(weights, moment):
    unit_rows = moment * lax.rsqrt(lax.optimization_barrier(jnp.mean(moment * moment, axis=-1, keepdims=True)) + 1e-05)
    moved = weights + step_size * unit_rows
    old_sq = lax.optimization_barrier(jnp.mean(weights * weights, axis=-1, keepdims=True)) + 1e-06
    new_sq = lax.optimization_barrier(jnp.mean(moved * moved, axis=-1, keepdims=True)) + 1e-06
    return moved * jnp.sqrt(old_sq / new_sq)

def reference(queries, key_vectors, value_vectors, token_rates, fast_init, out_proj):
    results = []
    weights_all = [fast_init[head_idx].astype(jnp.float32) for head_idx in range(HEADS)]
    moments = [jnp.zeros((3, HD, HD), jnp.float32) for head_idx in range(HEADS)]
    for block_idx in range(BLOCKS):
        mixed_out = jnp.zeros((CTOK, D), jnp.float32)
        for head_idx in range(HEADS):
            weights_bf = weights_all[head_idx].astype(jnp.bfloat16)
            grads = fast_grads(weights_bf, key_vectors[block_idx, :, head_idx], value_vectors[block_idx, :, head_idx], token_rates[block_idx, :, head_idx])
            moments[head_idx] = momentum_beta * moments[head_idx] + grads
            weights_all[head_idx] = renorm(weights_all[head_idx], moments[head_idx])
            head_out = fast_apply(weights_all[head_idx].astype(jnp.bfloat16), queries[block_idx, :, head_idx])
            mixed_out = mixed_out + jnp.dot(head_out, out_proj[head_idx], preferred_element_type=jnp.float32)
        results.append(mixed_out.astype(jnp.bfloat16))
    return jnp.stack(results)
```

```python
import functools

import jax
import jax.numpy as jnp
from jax import lax
from jax.experimental import pallas as pl
from jax.experimental.pallas import tpu as pltpu
from jax.sharding import PartitionSpec as P

momentum_beta = 0.9
step_size = 0.03
f32 = jnp.float32
bf16 = jnp.bfloat16
VMEM = pl.BlockSpec(memory_space=pltpu.VMEM)
SMEM = pl.BlockSpec(memory_space=pltpu.SMEM)


def params(mib=40):
    return pltpu.CompilerParams(vmem_limit_bytes=mib * 2**20)


def dot(x, y, contract=((1,), (0,))):
    return lax.dot_general(x, y, (contract, ((), ())), preferred_element_type=f32)


def sigmoid(x):
    return 0.5 * jnp.tanh(0.5 * x) + 0.5


def assemble(me, shard_refs, full):
    shards = len(shard_refs)
    rows = full.shape[1] // shards
    for j, ref in enumerate(shard_refs):
        place = pl.ds(pl.multiple_of((me ^ j) * rows, rows), rows)
        for m in range(full.shape[0]):
            full[m, place, :] = ref[m * rows : (m + 1) * rows, :]


def grads_kernel(shards, first, me_ref, k_ref, v_ref, r_ref, *refs):
    n_w = 1 if first else shards
    w_refs, out_refs = refs[:n_w], refs[n_w : n_w + shards]
    scratch = refs[n_w + shards :]
    da_s, db_s, hid_s, dy_s, g_s = scratch[:5]
    me = me_ref[0]
    if first:
        w = w_refs[0]
    else:
        w = scratch[5]
        assemble(me, w_refs, w)
    tok, width = k_ref.shape
    rate_col = jnp.broadcast_to(r_ref[...], (8, tok)).T[:, :1]
    chunk = min(tok, 256)
    for t in range(0, tok, chunk):
        span = slice(t, t + chunk)
        k = k_ref[span, :]
        a = dot(k, w[0])
        b = dot(k, w[1])
        sig = sigmoid(a)
        silu = a * sig
        hid_s[span, :] = (silu * b).astype(bf16)
        dy = (rate_col[span] * v_ref[span, :].astype(f32)).astype(bf16)
        dy_s[span, :] = dy
        dh = dot(dy, w[2], ((1,), (1,)))
        da_s[span, :] = (dh * b * sig * (1.0 + a * (1.0 - sig))).astype(bf16)
        db_s[span, :] = (dh * silu).astype(bf16)
    over_tokens = ((0,), (0,))
    g_s[0] = dot(k_ref[...], da_s[...], over_tokens).astype(bf16)
    g_s[1] = dot(k_ref[...], db_s[...], over_tokens).astype(bf16)
    g_s[2] = dot(hid_s[...], dy_s[...], over_tokens).astype(bf16)
    rows = width // shards
    for j, out in enumerate(out_refs):
        place = pl.ds(pl.multiple_of((me ^ j) * rows, rows), rows)
        for m in range(3):
            out[m * rows : (m + 1) * rows, :] = g_s[m, place, :]


def local_grads(me, k, v, r, w):
    first = len(w) == 1
    tok, width = k.shape
    shards = SHARDS if first else len(w)
    rows = 3 * width // shards
    scratch = [pltpu.VMEM((tok, width), bf16)] * 4 + [pltpu.VMEM((3, width, width), bf16)]
    if not first:
        scratch.append(pltpu.VMEM((3, width, width), bf16))
    return pl.pallas_call(
        functools.partial(grads_kernel, shards, first),
        out_shape=[jax.ShapeDtypeStruct((rows, width), bf16)] * shards,
        in_specs=[SMEM] + [VMEM] * (3 + len(w)),
        out_specs=[VMEM] * shards,
        scratch_shapes=scratch,
        compiler_params=params(),
        name="grads",
    )(me, k, v, r, *w)


def sum_kernel(*refs):
    total = refs[0][...].astype(f32)
    for ref in refs[1:-1]:
        total = total + ref[...].astype(f32)
    refs[-1][...] = total.astype(bf16)


def sum_parts(parts):
    return pl.pallas_call(
        sum_kernel,
        out_shape=jax.ShapeDtypeStruct(parts[0].shape, bf16),
        in_specs=[VMEM] * len(parts),
        out_specs=VMEM,
        compiler_params=params(),
        name="sum_parts",
    )(*parts)


def update_kernel(first, me_ref, p_ref, q_ref, *refs):
    grad = p_ref[...].astype(f32) + q_ref[...].astype(f32)
    if first:
        init_ref, w_out, m_out, wb_out, w_s = refs
        rows = p_ref.shape[0] // 3
        place = pl.ds(pl.multiple_of(me_ref[0] * rows, rows), rows)
        for m in range(3):
            w_s[m * rows : (m + 1) * rows, :] = init_ref[m, place, :]
        weights = w_s[...].astype(f32)
        moment = grad
    else:
        w_ref, m_ref, wb_out = refs
        weights = w_ref[...]
        moment = momentum_beta * m_ref[...] + grad
    unit = moment * lax.rsqrt(jnp.mean(moment * moment, axis=-1, keepdims=True) + 1e-05)
    moved = weights + step_size * unit
    old_sq = jnp.mean(weights * weights, axis=-1, keepdims=True) + 1e-06
    new_sq = jnp.mean(moved * moved, axis=-1, keepdims=True) + 1e-06
    weights = moved * jnp.sqrt(old_sq / new_sq)
    wb_out[...] = weights.astype(bf16)
    if first:
        w_out[...] = weights
        m_out[...] = moment


def update_first(me, p, q, init):
    shape = p.shape
    return pl.pallas_call(
        functools.partial(update_kernel, True),
        out_shape=[
            jax.ShapeDtypeStruct(shape, f32),
            jax.ShapeDtypeStruct(shape, f32),
            jax.ShapeDtypeStruct(shape, bf16),
        ],
        in_specs=[SMEM] + [VMEM] * 3,
        out_specs=[VMEM] * 3,
        scratch_shapes=[pltpu.VMEM(shape, bf16)],
        compiler_params=params(),
        name="update_first",
    )(me, p, q, init)


def update_next(me, p, q, weights, moment):
    return pl.pallas_call(
        functools.partial(update_kernel, False),
        out_shape=jax.ShapeDtypeStruct(p.shape, bf16),
        in_specs=[SMEM] + [VMEM] * 4,
        out_specs=VMEM,
        compiler_params=params(),
        name="update_next",
    )(me, p, q, weights, moment)


def apply_kernel(shards, me_ref, q_ref, *refs):
    w_refs, out, w = refs[:shards], refs[shards], refs[shards + 1]
    assemble(me_ref[0], w_refs, w)
    tok = q_ref.shape[0]
    chunk = min(tok, 256)
    for t in range(0, tok, chunk):
        span = slice(t, t + chunk)
        q = q_ref[span, :]
        a = dot(q, w[0])
        b = dot(q, w[1])
        hid = (a * sigmoid(a) * b).astype(bf16)
        out[span, :] = dot(hid, w[2]).astype(bf16)


def fast_apply(me, q, w):
    width = q.shape[1]
    return pl.pallas_call(
        functools.partial(apply_kernel, len(w)),
        out_shape=jax.ShapeDtypeStruct(q.shape, bf16),
        in_specs=[SMEM] + [VMEM] * (1 + len(w)),
        out_specs=VMEM,
        scratch_shapes=[pltpu.VMEM((3, width, width), bf16)],
        compiler_params=params(),
        name="apply",
    )(me, q, *w)


def project_kernel(o_ref, other_ref, proj_ref, proj_other_ref, *refs):
    out = refs[-1]
    out[0] = (dot(o_ref[...], proj_ref[...]) + dot(other_ref[...], proj_other_ref[...])).astype(bf16)


def project(block, blocks, o, o_other, proj, proj_other, into):
    tok, width = o.shape
    cols = proj.shape[1]
    part = min(cols, 256)
    whole = pl.BlockSpec((tok, width), lambda i: (0, 0))
    columns = pl.BlockSpec((width, part), lambda i: (0, i))
    args = [o, o_other, proj, proj_other]
    specs = [whole, whole, columns, columns]
    aliases = {}
    if into is not None:
        args.append(into)
        specs.append(pl.BlockSpec(memory_space=pl.ANY))
        aliases = {4: 0}
    return pl.pallas_call(
        project_kernel,
        grid=(cols // part,),
        out_shape=jax.ShapeDtypeStruct((blocks, tok, cols), bf16),
        in_specs=specs,
        out_specs=pl.BlockSpec((1, tok, part), lambda i: (block, 0, i)),
        input_output_aliases=aliases,
        compiler_params=params(),
        name="project",
    )(*args)


SHARDS = 8


def solution(mesh):
    ctx, heads = mesh.shape["ctx"], mesh.shape["head"]
    assert ctx & (ctx - 1) == 0 and ctx >= SHARDS and heads == 2

    def swap(x, bit):
        return lax.ppermute(x, "ctx", [(i, i ^ bit) for i in range(ctx)])

    def swap_head(x):
        return lax.ppermute(x, "head", [(0, 1), (1, 0)])

    order = (1, 2, 4, 3, 5, 6, 7)

    def reduce_parts(parts):
        got = {j: swap(parts[j], j) for j in order}
        p = sum_parts([parts[0]] + [got[j] for j in order])
        bit = SHARDS
        while bit < ctx // 2:
            p = sum_parts([p, swap(p, bit)])
            bit *= 2
        return p, (swap(p, bit) if bit < ctx else jnp.zeros_like(p))

    def gather(part):
        got = {j: swap(part, j) for j in order}
        return [part] + [got[j] for j in range(1, SHARDS)]

    def on_device(queries, key_vectors, value_vectors, token_rates, fast_init, out_proj):
        blocks, tok, _, width = queries.shape
        flat = lambda x: x.reshape(blocks, tok, width)
        q, k, v = flat(queries), flat(key_vectors), flat(value_vectors)
        r = token_rates.reshape(blocks, 1, tok)
        init, proj_all = fast_init[0], out_proj[0]
        me = (lax.axis_index("ctx") % SHARDS).astype(jnp.int32).reshape(1)
        half = proj_all.shape[1] // heads
        head = lax.axis_index("head")
        proj = lax.dynamic_slice_in_dim(proj_all, head * half, half, 1)
        proj_other = swap_head(lax.dynamic_slice_in_dim(proj_all, (1 - head) * half, half, 1))

        result = None
        w = [init]
        weights = moment = None
        for c in range(blocks):
            p, p_other = reduce_parts(local_grads(me, k[c], v[c], r[c], w))
            if c == 0:
                weights, moment, wb = update_first(me, p, p_other, init)
            else:
                wb = update_next(me, p, p_other, weights, moment)
            w = gather(wb)
            o = fast_apply(me, q[c], w)
            result = project(c, blocks, o, swap_head(o), proj, proj_other, result)
        return result

    placed = (
        P(None, "ctx", "head", None),
        P(None, "ctx", "head", None),
        P(None, "ctx", "head", None),
        P(None, "ctx", "head"),
        P("head", None, None, None),
        P("head", None, None),
    )
    return jax.shard_map(on_device, mesh=mesh, in_specs=placed, out_specs=P(None, "ctx", "head"), check_vma=False)
```

```python
import functools

import jax
import jax.numpy as jnp
from jax import lax
from jax.experimental import pallas as pl
from jax.experimental.pallas import tpu as pltpu
from jax.sharding import PartitionSpec as P

momentum_beta = 0.9
step_size = 0.03
f32 = jnp.float32
bf16 = jnp.bfloat16
VMEM = pl.BlockSpec(memory_space=pltpu.VMEM)
SMEM = pl.BlockSpec(memory_space=pltpu.SMEM)


def params(mib=40):
    return pltpu.CompilerParams(vmem_limit_bytes=mib * 2**20)


def dot(x, y, contract=((1,), (0,))):
    return lax.dot_general(x, y, (contract, ((), ())), preferred_element_type=f32)


def sigmoid(x):
    return 0.5 * jnp.tanh(0.5 * x) + 0.5


def base_row(owner, width):
    return ((owner % 2) * (SHARDS // 2) + owner // 2) * (width // SHARDS)


def pieces_of(chunk, mine):
    found = [(i, 0, r) for i, r in enumerate((0, 2, 4, 6))]
    return found + [(4, i * mine, r) for i, r in enumerate((1, 3, 5, 7))]


def assemble(me, refs, full):
    width = full.shape[1]
    chunks = len(refs) // 5
    rows = width // SHARDS // chunks
    for h in range(chunks):
        for i, first, r in pieces_of(h, 3 * rows):
            ref = refs[5 * h + i]
            place = pl.ds(pl.multiple_of(base_row(me ^ r, width) + h * rows, rows), rows)
            for m in range(3):
                full[m, place, :] = ref[first + m * rows : first + (m + 1) * rows, :]


def grads_kernel(first, me_ref, k_ref, v_ref, r_ref, *refs):
    n_w = 1 if first else 5 * CHUNKS
    w_refs, out_refs = refs[:n_w], refs[n_w : n_w + 2 * CHUNKS]
    scratch = refs[n_w + 2 * CHUNKS :]
    da_s, db_s, hid_s, dy_s, g_s = scratch[:5]
    me = me_ref[0]
    if first:
        w = w_refs[0]
    else:
        w = scratch[5]
        assemble(me, w_refs, w)
    tok, width = k_ref.shape
    rate_col = jnp.broadcast_to(r_ref[...], (8, tok)).T[:, :1]
    chunk = min(tok, 256)
    for t in range(0, tok, chunk):
        span = slice(t, t + chunk)
        k = k_ref[span, :]
        a = dot(k, w[0])
        b = dot(k, w[1])
        sig = sigmoid(a)
        silu = a * sig
        hid_s[span, :] = (silu * b).astype(bf16)
        dy = (rate_col[span] * v_ref[span, :].astype(f32)).astype(bf16)
        dy_s[span, :] = dy
        dh = dot(dy, w[2], ((1,), (1,)))
        da_s[span, :] = (dh * b * sig * (1.0 + a * (1.0 - sig))).astype(bf16)
        db_s[span, :] = (dh * silu).astype(bf16)
    over_tokens = ((0,), (0,))
    g_s[0] = dot(k_ref[...], da_s[...], over_tokens).astype(bf16)
    g_s[1] = dot(k_ref[...], db_s[...], over_tokens).astype(bf16)
    g_s[2] = dot(hid_s[...], dy_s[...], over_tokens).astype(bf16)
    rows = width // SHARDS // CHUNKS
    for h in range(CHUNKS):
        for out, relative in ((out_refs[2 * h], (1, 3, 5, 7)), (out_refs[2 * h + 1], (0, 2, 4, 6))):
            for i, r in enumerate(relative):
                place = pl.ds(pl.multiple_of(base_row(me ^ r, width) + h * rows, rows), rows)
                for m in range(3):
                    row = (3 * i + m) * rows
                    out[row : row + rows, :] = g_s[m, place, :]


def local_grads(me, k, v, r, block, w):
    first = len(w) == 1
    _, tok, width = k.shape
    rows = 3 * width // 2 // CHUNKS
    scratch = [pltpu.VMEM((tok, width), bf16)] * 4 + [pltpu.VMEM((3, width, width), bf16)]
    if not first:
        scratch.append(pltpu.VMEM((3, width, width), bf16))
    of_block = lambda *shape: pl.BlockSpec((None, *shape), lambda i: (block, 0, 0))
    return pl.pallas_call(
        functools.partial(grads_kernel, first),
        grid=(1,),
        out_shape=[jax.ShapeDtypeStruct((rows, width), bf16)] * (2 * CHUNKS),
        in_specs=[SMEM, of_block(tok, width), of_block(tok, width), of_block(1, tok)] + [VMEM] * len(w),
        out_specs=[VMEM] * (2 * CHUNKS),
        scratch_shapes=scratch,
        compiler_params=params(),
        name="grads",
    )(me, k, v, r, *w)


def update_kernel(first, chunk, keep, me_ref, p_ref, q_ref, *refs):
    grad = p_ref[...].astype(f32) + q_ref[...].astype(f32)
    if first:
        init_ref, *refs, w_s = refs
        width = init_ref.shape[1]
        rows = p_ref.shape[0] // 3
        place = pl.ds(pl.multiple_of(base_row(me_ref[0], width) + chunk * rows, rows), rows)
        for m in range(3):
            w_s[m * rows : (m + 1) * rows, :] = init_ref[m, place, :]
        weights = w_s[...].astype(f32)
        moment = grad
    else:
        w_ref, m_ref, *refs = refs
        weights = w_ref[...]
        moment = momentum_beta * m_ref[...] + grad
    unit = moment * lax.rsqrt(jnp.mean(moment * moment, axis=-1, keepdims=True) + 1e-05)
    moved = weights + step_size * unit
    old_sq = jnp.mean(weights * weights, axis=-1, keepdims=True) + 1e-06
    new_sq = jnp.mean(moved * moved, axis=-1, keepdims=True) + 1e-06
    weights = moved * jnp.sqrt(old_sq / new_sq)
    refs[0][...] = weights.astype(bf16)
    if keep:
        refs[1][...] = weights
        refs[2][...] = moment


def update(me, p, q, chunk, state, init, keep):
    shape = p.shape
    first = state is None
    out = [jax.ShapeDtypeStruct(shape, bf16)] + [jax.ShapeDtypeStruct(shape, f32)] * (2 if keep else 0)
    state = [init] if first else state
    got = pl.pallas_call(
        functools.partial(update_kernel, first, chunk, keep),
        out_shape=out,
        in_specs=[SMEM] + [VMEM] * (2 + len(state)),
        out_specs=[VMEM] * len(out),
        scratch_shapes=[pltpu.VMEM(shape, bf16)] if first else [],
        compiler_params=params(),
        name="update",
    )(me, p, q, *state)
    return got[0], got[1:]


def apply_kernel(n_w, me_ref, q_ref, *refs):
    w_refs, out, w = refs[:n_w], refs[n_w], refs[n_w + 1]
    assemble(me_ref[0], w_refs, w)
    tok = q_ref.shape[0]
    chunk = min(tok, 256)
    for t in range(0, tok, chunk):
        span = slice(t, t + chunk)
        q = q_ref[span, :]
        a = dot(q, w[0])
        b = dot(q, w[1])
        hid = (a * sigmoid(a) * b).astype(bf16)
        out[span, :] = dot(hid, w[2]).astype(bf16)


def fast_apply(me, q, block, w):
    _, tok, width = q.shape
    return pl.pallas_call(
        functools.partial(apply_kernel, len(w)),
        grid=(1,),
        out_shape=jax.ShapeDtypeStruct((tok, width), bf16),
        in_specs=[SMEM, pl.BlockSpec((None, tok, width), lambda i: (block, 0, 0))] + [VMEM] * len(w),
        out_specs=VMEM,
        scratch_shapes=[pltpu.VMEM((3, width, width), bf16)],
        compiler_params=params(),
        name="apply",
    )(me, q, *w)


def project_kernel(o_ref, other_ref, proj_ref, proj_other_ref, *refs):
    out = refs[-1]
    out[0] = (dot(o_ref[...], proj_ref[...]) + dot(other_ref[...], proj_other_ref[...])).astype(bf16)


def project(block, blocks, o, o_other, proj, proj_other, into):
    tok, width = o.shape
    cols = proj.shape[1]
    part = min(cols, 256)
    whole = pl.BlockSpec((tok, width), lambda i: (0, 0))
    columns = pl.BlockSpec((width, part), lambda i: (0, i))
    args = [o, o_other, proj, proj_other]
    specs = [whole, whole, columns, columns]
    aliases = {}
    if into is not None:
        args.append(into)
        specs.append(pl.BlockSpec(memory_space=pl.ANY))
        aliases = {4: 0}
    return pl.pallas_call(
        project_kernel,
        grid=(cols // part,),
        out_shape=jax.ShapeDtypeStruct((blocks, tok, cols), bf16),
        in_specs=specs,
        out_specs=pl.BlockSpec((1, tok, part), lambda i: (block, 0, i)),
        input_output_aliases=aliases,
        compiler_params=params(),
        name="project",
    )(*args)


SHARDS = 8
CHUNKS = 2


def swap_low_bits(i):
    return (i & ~3) | ((i & 1) << 1) | ((i >> 1) & 1)


def tie(x, other):
    return lax.optimization_barrier((x, other))[0]


def solution(mesh):
    ctx, heads = mesh.shape["ctx"], mesh.shape["head"]
    assert ctx & (ctx - 1) == 0 and ctx >= SHARDS and heads == 2

    def swap(x, bits):
        pairs = [(2 * i, 2 * (i ^ bits)) for i in range(ctx)]
        pairs += [(2 * i + 1, 2 * (i ^ swap_low_bits(bits)) + 1) for i in range(ctx)]
        return lax.ppermute(x, ("ctx", "head"), pairs)

    def swap_head(x):
        return lax.ppermute(x, "head", [(0, 1), (1, 0)])

    def add(x, y):
        return x.astype(f32) + y.astype(f32)

    def reduce_chunk(send, keep):
        total = add(keep, swap(send, 1))
        n = total.shape[0] // 4
        mine = total[:n]
        for i, bits in ((2, 4), (3, 6), (1, 2)):
            mine = add(mine, swap(total[i * n : (i + 1) * n].astype(bf16), bits))
        p = mine.astype(bf16)
        bit = SHARDS
        while bit < ctx // 2:
            p = add(p, swap(p, bit)).astype(bf16)
            bit *= 2
        return p, (swap(p, bit) if bit < ctx else jnp.zeros_like(p))

    def gather(part):
        near = [part] + [swap(part, bits) for bits in (2, 4, 6)]
        return near + [swap(jnp.concatenate(near), 1)]

    def on_device(queries, key_vectors, value_vectors, token_rates, fast_init, out_proj):
        blocks, tok, _, width = queries.shape
        flat = lambda x: x.reshape(blocks, tok, width)
        q, k, v = flat(queries), flat(key_vectors), flat(value_vectors)
        r = token_rates.reshape(blocks, 1, tok)
        init, proj_all = fast_init[0], out_proj[0]
        head = lax.axis_index("head")
        label = (lax.axis_index("ctx") % SHARDS).astype(jnp.int32)
        me = jnp.where(head == 0, label, swap_low_bits(label)).reshape(1)
        half = proj_all.shape[1] // heads
        proj = lax.dynamic_slice_in_dim(proj_all, head * half, half, 1)
        proj_other = swap_head(lax.dynamic_slice_in_dim(proj_all, (1 - head) * half, half, 1))

        result = None
        w = [init]
        state = [None] * CHUNKS
        for c in range(blocks):
            grads = local_grads(me, k, v, r, c, w)
            w = []
            for h in range(CHUNKS):
                p, p_other = reduce_chunk(grads[2 * h], grads[2 * h + 1])
                wb, state[h] = update(me, p, p_other, h, state[h], init, c + 1 < blocks)
                w += gather(wb)
            o = fast_apply(me, q, c, w)
            result = project(c, blocks, o, swap_head(o), proj, proj_other, result)
        return result

    placed = (
        P(None, "ctx", "head", None),
        P(None, "ctx", "head", None),
        P(None, "ctx", "head", None),
        P(None, "ctx", "head"),
        P("head", None, None, None),
        P("head", None, None),
    )
    return jax.shard_map(on_device, mesh=mesh, in_specs=placed, out_specs=P(None, "ctx", "head"), check_vma=False)
```

```python
import functools

import jax
import jax.numpy as jnp
from jax import lax
from jax.experimental import pallas as pl
from jax.experimental.pallas import tpu as pltpu
from jax.sharding import PartitionSpec as P

momentum_beta = 0.9
step_size = 0.03
f32 = jnp.float32
bf16 = jnp.bfloat16
VMEM = pl.BlockSpec(memory_space=pltpu.VMEM)
HBM = pl.BlockSpec(memory_space=pltpu.HBM)
SMEM = pl.BlockSpec(memory_space=pltpu.SMEM)


def params(mib=24):
    return pltpu.CompilerParams(vmem_limit_bytes=mib * 2**20)


def in_hbm(x):
    return pltpu.with_memory_space_constraint(x, pltpu.HBM)


def dot(x, y, contract=((1,), (0,))):
    return lax.dot_general(x, y, (contract, ((), ())), preferred_element_type=f32)


def sigmoid(x):
    return 0.5 * jnp.tanh(0.5 * x) + 0.5


def base_row(owner, width):
    return ((owner % 2) * (SHARDS // 2) + owner // 2) * (width // SHARDS)


def pieces_of(chunk, mine):
    found = [(i, 0, r) for i, r in enumerate((0, 2, 4, 6))]
    return found + [(4, i * mine, r) for i, r in enumerate((1, 3, 5, 7))]


def assemble(me, refs, full):
    width = full.shape[1]
    chunks = len(refs) // 5
    rows = width // SHARDS // chunks
    for h in range(chunks):
        for i, first, r in pieces_of(h, 3 * rows):
            ref = refs[5 * h + i]
            place = pl.ds(pl.multiple_of(base_row(me ^ r, width) + h * rows, rows), rows)
            for m in range(3):
                full[m, place, :] = ref[first + m * rows : first + (m + 1) * rows, :]


def token_grads(k, dy, w, da_s, db_s, hid_s, at):
    tok = k.shape[0]
    chunk = min(tok, 256)
    for t in range(0, tok, chunk):
        rows, span = slice(t, t + chunk), slice(at + t, at + t + chunk)
        a = dot(k[rows, :], w[0])
        b = dot(k[rows, :], w[1])
        sig = sigmoid(a)
        silu = a * sig
        hid_s[span, :] = (silu * b).astype(bf16)
        dh = dot(dy[rows, :], w[2], ((1,), (1,)))
        da_s[span, :] = (dh * b * sig * (1.0 + a * (1.0 - sig))).astype(bf16)
        db_s[span, :] = (dh * silu).astype(bf16)


def first_grads_kernel(me_ref, k_hbm, v_hbm, r_ref, w_hbm, *refs):
    out_refs, w0_refs = refs[: 2 * CHUNKS], refs[2 * CHUNKS : 3 * CHUNKS]
    k_s, v_s, w, da_s, db_s, hid_s, dy_s, g_s, sems = refs[3 * CHUNKS :]
    copies = [pltpu.make_async_copy(k_hbm.at[0], k_s, sems.at[0]), pltpu.make_async_copy(v_hbm.at[0], v_s, sems.at[1])]
    copies += [pltpu.make_async_copy(w_hbm.at[m], w.at[m], sems.at[2 + m]) for m in range(3)]
    for i in (1, 0, 2, 3, 4):
        copies[i].start()
    me = me_ref[0]
    tok, width = k_s.shape
    rate_col = jnp.broadcast_to(r_ref[...], (8, tok)).T[:, :1]
    copies[1].wait()
    dy_s[...] = (rate_col * v_s[...].astype(f32)).astype(bf16)
    for i in (0, 2, 3, 4):
        copies[i].wait()
    token_grads(k_s, dy_s, w, da_s, db_s, hid_s, 0)
    over_tokens = ((0,), (0,))
    g_s[0] = dot(k_s[...], da_s[...], over_tokens).astype(bf16)
    g_s[1] = dot(k_s[...], db_s[...], over_tokens).astype(bf16)
    g_s[2] = dot(hid_s[...], dy_s[...], over_tokens).astype(bf16)
    rows = width // SHARDS // CHUNKS
    for h in range(CHUNKS):
        for out, relative in ((out_refs[2 * h], (1, 3, 5, 7)), (out_refs[2 * h + 1], (0, 2, 4, 6))):
            for i, r in enumerate(relative):
                place = pl.ds(pl.multiple_of(base_row(me ^ r, width) + h * rows, rows), rows)
                for m in range(3):
                    row = (3 * i + m) * rows
                    out[row : row + rows, :] = g_s[m, place, :]
        place = pl.ds(pl.multiple_of(base_row(me, width) + h * rows, rows), rows)
        for m in range(3):
            w0_refs[h][m * rows : (m + 1) * rows, :] = w[m, place, :]


def first_grads(me, k, v, r, init):
    _, tok, width = k.shape
    rows = 3 * width // 2 // CHUNKS
    square = pltpu.VMEM((tok, width), bf16)
    weights = pltpu.VMEM((3, width, width), bf16)
    return pl.pallas_call(
        first_grads_kernel,
        grid=(1,),
        out_shape=[jax.ShapeDtypeStruct((rows, width), bf16)] * (2 * CHUNKS)
        + [jax.ShapeDtypeStruct((rows // 4, width), bf16)] * CHUNKS,
        in_specs=[SMEM, HBM, HBM, pl.BlockSpec((None, 1, tok), lambda i: (0, 0, 0)), HBM],
        out_specs=[VMEM] * (3 * CHUNKS),
        scratch_shapes=[square, square, weights, square, square, square, square, weights, pltpu.SemaphoreType.DMA((5,))],
        compiler_params=params(),
        name="first_grads",
    )(me, in_hbm(k), in_hbm(v), r, in_hbm(init))


def next_grads_kernel(n_w, me_ref, own_hbm, other_hbm, *refs):
    w_refs, out_refs, w_out = refs[:n_w], refs[n_w : n_w + 4 * CHUNKS], refs[n_w + 4 * CHUNKS]
    tok_s, da_s, db_s, hid_s, g_s, w, sems = refs[n_w + 4 * CHUNKS + 1 :]
    loads = [pltpu.make_async_copy(ref, tok_s.at[i], sems.at[i]) for i, ref in enumerate((own_hbm, other_hbm))]
    for load in loads:
        load.start()
    me = me_ref[0]
    assemble(me, w_refs, w)
    keep_w = pltpu.make_async_copy(w, w_out, sems.at[2])
    keep_w.start()
    tok, width = tok_s.shape[2:]
    half = width // 2
    for i, load in enumerate(loads):
        load.wait()
        token_grads(tok_s.at[i, 0], tok_s.at[i, 1], w, da_s, db_s, hid_s, i * tok)
    mine = pl.ds(pl.multiple_of((me % 2) * half, half), half)
    over_tokens = ((0,), (0,))
    spans = ((0, slice(0, tok)), (1, slice(tok, 2 * tok)))
    for m, d_s in ((0, da_s), (1, db_s)):
        g_s[m] = sum(dot(tok_s[i, 0, :, mine], d_s[span, :], over_tokens) for i, span in spans).astype(bf16)
    g_s[2] = sum(dot(hid_s[span, mine], tok_s[i, 1], over_tokens) for i, span in spans).astype(bf16)
    rows = width // SHARDS // CHUNKS
    for h in range(CHUNKS):
        for i, r in enumerate((0, 2, 4, 6)):
            place = pl.ds(pl.multiple_of((me ^ r) // 2 * (rows * CHUNKS) + h * rows, rows), rows)
            for m in range(3):
                out_refs[4 * h + i][m * rows : (m + 1) * rows, :] = g_s[m, place, :]
    keep_w.wait()


def next_grads(me, own, other, w):
    _, tok, width = own.shape
    rows = 3 * width // SHARDS // CHUNKS
    return pl.pallas_call(
        functools.partial(next_grads_kernel, len(w)),
        out_shape=[jax.ShapeDtypeStruct((rows, width), bf16)] * (4 * CHUNKS) + [pltpu.HBM((3, width, width), bf16)],
        in_specs=[SMEM, HBM, HBM] + [VMEM] * len(w),
        out_specs=[VMEM] * (4 * CHUNKS) + [HBM],
        scratch_shapes=[pltpu.VMEM((2, 2, tok, width), bf16)]
        + [pltpu.VMEM((2 * tok, width), bf16)] * 3
        + [pltpu.VMEM((3, width // 2, width), bf16), pltpu.VMEM((3, width, width), bf16), pltpu.SemaphoreType.DMA((3,))],
        compiler_params=params(),
        name="next_grads",
    )(me, in_hbm(own), in_hbm(other), *w)


def update_kernel(keep, p_ref, q_ref, w_ref, *refs):
    moment = p_ref[...].astype(f32) + q_ref[...].astype(f32)
    weights = w_ref[...].astype(f32)
    n_out = 3 if keep else 1
    if len(refs) > n_out:
        moment = momentum_beta * refs[0][...] + moment
    outs = refs[-n_out:]
    unit = moment * lax.rsqrt(jnp.mean(moment * moment, axis=-1, keepdims=True) + 1e-05)
    moved = weights + step_size * unit
    old_sq = jnp.mean(weights * weights, axis=-1, keepdims=True) + 1e-06
    new_sq = jnp.mean(moved * moved, axis=-1, keepdims=True) + 1e-06
    weights = moved * jnp.sqrt(old_sq / new_sq)
    outs[0][...] = weights.astype(bf16)
    if keep:
        outs[1][...] = weights
        outs[2][...] = moment


def update(p, q, state, keep):
    out = [jax.ShapeDtypeStruct(p.shape, bf16)] + [jax.ShapeDtypeStruct(p.shape, f32)] * (2 if keep else 0)
    got = pl.pallas_call(
        functools.partial(update_kernel, keep),
        out_shape=out,
        in_specs=[VMEM] * (2 + len(state)),
        out_specs=[VMEM] * len(out),
        compiler_params=params(),
        name="update",
    )(p, q, *state)
    return got[0], got[1:]


def apply_kernel(n_w, me_ref, q_ref, *refs):
    w_refs, out = refs[:n_w], refs[n_w]
    if n_w == 1:
        w = w_refs[0]
    else:
        w = refs[n_w + 1]
        assemble(me_ref[0], w_refs, w)
    tok = q_ref.shape[0]
    chunk = min(tok, 256)
    for t in range(0, tok, chunk):
        span = slice(t, t + chunk)
        q = q_ref[span, :]
        a = dot(q, w[0])
        b = dot(q, w[1])
        hid = (a * sigmoid(a) * b).astype(bf16)
        out[span, :] = dot(hid, w[2]).astype(bf16)


def fast_apply(me, q, block, w):
    _, tok, width = q.shape
    whole = pl.BlockSpec((3, width, width), lambda i: (0, 0, 0))
    return pl.pallas_call(
        functools.partial(apply_kernel, len(w)),
        grid=(1,),
        out_shape=jax.ShapeDtypeStruct((tok, width), bf16),
        in_specs=[SMEM, pl.BlockSpec((None, tok, width), lambda i: (block, 0, 0))] + ([whole] if len(w) == 1 else [VMEM] * len(w)),
        out_specs=VMEM,
        scratch_shapes=[pltpu.VMEM((3, width, width), bf16)] if len(w) > 1 else [],
        compiler_params=params(),
        name="apply",
    )(me, q, *w)


def project_own_kernel(o_ref, proj_ref, out):
    out[...] = dot(o_ref[...], proj_ref[...])


def project_own(o, proj):
    return pl.pallas_call(
        project_own_kernel,
        out_shape=jax.ShapeDtypeStruct((o.shape[0], proj.shape[1]), f32),
        in_specs=[VMEM] * 2,
        out_specs=VMEM,
        compiler_params=params(),
        name="project_own",
    )(o, proj)


def project_kernel(sum_ref, o_ref, proj_ref, *refs):
    refs[-1][...] = (sum_ref[...] + dot(o_ref[...], proj_ref[...])).astype(bf16)


def project(block, blocks, own, o_other, proj_other, into):
    tok, width = o_other.shape
    cols = proj_other.shape[1]
    args = [own, o_other, proj_other]
    specs = [pl.BlockSpec(x.shape, lambda i: (0, 0)) for x in args]
    aliases = {}
    if into is not None:
        args.append(into)
        specs.append(pl.BlockSpec(memory_space=pl.ANY))
        aliases = {3: 0}
    return pl.pallas_call(
        project_kernel,
        grid=(1,),
        out_shape=jax.ShapeDtypeStruct((blocks, tok, cols), bf16),
        in_specs=specs,
        out_specs=pl.BlockSpec((None, tok, cols), lambda i: (block, 0, 0)),
        input_output_aliases=aliases,
        compiler_params=params(),
        name="project",
    )(*args)


SHARDS = 8
CHUNKS = 2


def swap_low_bits(i):
    return (i & ~3) | ((i & 1) << 1) | ((i >> 1) & 1)


def together(*values):
    return lax.optimization_barrier(values)


def solution(mesh):
    ctx, heads = mesh.shape["ctx"], mesh.shape["head"]
    assert ctx & (ctx - 1) == 0 and ctx >= SHARDS and heads == 2

    def swap(x, bits):
        pairs = [(2 * i, 2 * (i ^ bits)) for i in range(ctx)]
        pairs += [(2 * i + 1, 2 * (i ^ swap_low_bits(bits)) + 1) for i in range(ctx)]
        return lax.ppermute(x, ("ctx", "head"), pairs)

    def swap_head(x):
        return lax.ppermute(x, "head", [(0, 1), (1, 0)])

    def add(x, y):
        return x.astype(f32) + y.astype(f32)

    def reduce_half(send, keep):
        total = add(keep, swap(send, 1))
        n = total.shape[0] // 4
        return [total[i * n : (i + 1) * n] for i in range(4)]

    def reduce_pieces(pieces):
        mine = pieces[0]
        for i, bits in ((2, 4), (3, 6), (1, 2)):
            mine = add(mine, swap(pieces[i].astype(bf16), bits))
        p = mine.astype(bf16)
        bit = SHARDS
        while bit < ctx // 2:
            p = add(p, swap(p, bit)).astype(bf16)
            bit *= 2
        return p

    def last_exchange(p):
        return swap(p, ctx // 2) if ctx > SHARDS else jnp.zeros_like(p)

    def gather_near(part):
        return [part] + [swap(part, bits) for bits in (2, 4, 6)]

    def on_device(queries, key_vectors, value_vectors, token_rates, fast_init, out_proj):
        blocks, tok, _, width = queries.shape
        flat = lambda x: x.reshape(blocks, tok, width)
        q, k, v = flat(queries), flat(key_vectors), flat(value_vectors)
        r = token_rates.reshape(blocks, 1, tok)
        init, proj_all = fast_init[0], out_proj[0]
        head = lax.axis_index("head")
        label = (lax.axis_index("ctx") % SHARDS).astype(jnp.int32)
        me = jnp.where(head == 0, label, swap_low_bits(label)).reshape(1)
        half = proj_all.shape[1] // heads
        proj = lax.dynamic_slice_in_dim(proj_all, head * half, half, 1)
        proj_other = swap_head(lax.dynamic_slice_in_dim(proj_all, (1 - head) * half, half, 1))

        def finish(c, me, w, into):
            o = fast_apply(me, q, c, w)
            return project(c, blocks, project_own(o, proj), swap_head(o), proj_other, into)

        result = None
        for c in range(blocks):
            if c == 0:
                grads = first_grads(me, k, v, r, init)
                state = [[w0] for w0 in grads[2 * CHUNKS :]]
                pieces = [reduce_half(*grads[2 * h : 2 * h + 2]) for h in range(CHUNKS)]
            else:
                grads = next_grads(me, tokens, tokens_other, w)
                pieces = [grads[4 * h : 4 * h + 4] for h in range(CHUNKS)]
            near = []
            for h in range(CHUNKS):
                p = reduce_pieces(pieces[h])
                if h == 0 and c + 1 < blocks:
                    dy = (r[c + 1, 0][:, None] * v[c + 1].astype(f32)).astype(bf16)
                    tokens = jnp.stack([k[c + 1], dy])
                    p, sent = together(p, tokens)
                    tokens_other = swap(sent, 1)
                wb, state[h] = update(p, last_exchange(p), state[h], c + 1 < blocks)
                near.append(gather_near(wb))
            joined = [jnp.concatenate(pieces) for pieces in near]
            if c > 0:
                joined[-1], me = together(joined[-1], me)
                result = finish(c - 1, me, grads[4 * CHUNKS :], result)
                me, result = together(me, result)
            w = [x for pieces, all_near in zip(near, joined) for x in (*pieces, swap(all_near, 1))]
        return finish(blocks - 1, me, w, result)

    placed = (
        P(None, "ctx", "head", None),
        P(None, "ctx", "head", None),
        P(None, "ctx", "head", None),
        P(None, "ctx", "head"),
        P("head", None, None, None),
        P("head", None, None),
    )
    return jax.shard_map(on_device, mesh=mesh, in_specs=placed, out_specs=P(None, "ctx", "head"), check_vma=False)
```

```python
import functools

import jax
import jax.numpy as jnp
from jax import lax
from jax.experimental import pallas as pl
from jax.experimental.pallas import tpu as pltpu
from jax.sharding import PartitionSpec as P

momentum_beta = 0.9
step_size = 0.03
f32 = jnp.float32
bf16 = jnp.bfloat16
VMEM = pl.BlockSpec(memory_space=pltpu.VMEM)
HBM = pl.BlockSpec(memory_space=pltpu.HBM)
SMEM = pl.BlockSpec(memory_space=pltpu.SMEM)


def params(mib=24):
    return pltpu.CompilerParams(vmem_limit_bytes=mib * 2**20)


def in_hbm(x):
    return pltpu.with_memory_space_constraint(x, pltpu.HBM)


def dot(x, y, contract=((1,), (0,))):
    return lax.dot_general(x, y, (contract, ((), ())), preferred_element_type=f32)


def sigmoid(x):
    return 0.5 * jnp.tanh(0.5 * x) + 0.5


def base_row(owner, width):
    return ((owner % 2) * (SHARDS // 2) + owner // 2) * (width // SHARDS)


def pieces_of(chunk, mine):
    found = [(i, 0, r) for i, r in enumerate((0, 2, 4, 6))]
    return found + [(4, i * mine, r) for i, r in enumerate((1, 3, 5, 7))]


def assemble(me, refs, full):
    width = full.shape[1]
    chunks = len(refs) // 5
    rows = width // SHARDS // chunks
    for h in range(chunks):
        for i, first, r in pieces_of(h, 3 * rows):
            ref = refs[5 * h + i]
            place = pl.ds(pl.multiple_of(base_row(me ^ r, width) + h * rows, rows), rows)
            for m in range(3):
                full[m, place, :] = ref[first + m * rows : first + (m + 1) * rows, :]


def token_grads(k, dy, w, da_s, db_s, hid_s, at, ready=lambda name: None):
    tok = k.shape[0]
    chunk = min(tok, 512)
    for t in range(0, tok, chunk):
        rows, span = slice(t, t + chunk), slice(at + t, at + t + chunk)
        if t == 0:
            ready("gate")
        a = dot(k[rows, :], w[0])
        if t == 0:
            ready("linear")
        b = dot(k[rows, :], w[1])
        sig = sigmoid(a)
        silu = a * sig
        hid_s[span, :] = (silu * b).astype(bf16)
        if t == 0:
            ready("output")
        dh = dot(dy[rows, :], w[2], ((1,), (1,)))
        da_s[span, :] = (dh * (b * (sig + silu * (1.0 - sig)))).astype(bf16)
        db_s[span, :] = (dh * silu).astype(bf16)


def first_grads_kernel(me_ref, k_hbm, v_hbm, r_ref, w_hbm, *refs):
    out_refs, w0_refs = refs[: 2 * CHUNKS], refs[2 * CHUNKS : 3 * CHUNKS]
    k_s, v_s, w, da_s, db_s, hid_s, dy_s, g_s, sems = refs[3 * CHUNKS :]
    copies = [pltpu.make_async_copy(k_hbm.at[0], k_s, sems.at[0]), pltpu.make_async_copy(v_hbm.at[0], v_s, sems.at[1])]
    copies += [pltpu.make_async_copy(w_hbm.at[m], w.at[m], sems.at[2 + m]) for m in range(3)]
    for i in (0, 2, 3, 1, 4):
        copies[i].start()
    me = me_ref[0]
    tok, width = k_s.shape
    rate_col = jnp.broadcast_to(r_ref[...], (8, tok)).T[:, :1]

    def ready(name):
        for i in {"gate": (0, 2), "linear": (3,), "output": (1, 4)}[name]:
            copies[i].wait()
        if name == "output":
            dy_s[...] = (rate_col * v_s[...].astype(f32)).astype(bf16)

    token_grads(k_s, dy_s, w, da_s, db_s, hid_s, 0, ready)
    over_tokens = ((0,), (0,))
    g_s[0] = dot(k_s[...], da_s[...], over_tokens).astype(bf16)
    g_s[1] = dot(k_s[...], db_s[...], over_tokens).astype(bf16)
    g_s[2] = dot(hid_s[...], dy_s[...], over_tokens).astype(bf16)
    rows = width // SHARDS // CHUNKS
    for h in range(CHUNKS):
        for out, relative in ((out_refs[2 * h], (1, 3, 5, 7)), (out_refs[2 * h + 1], (0, 2, 4, 6))):
            for i, r in enumerate(relative):
                place = pl.ds(pl.multiple_of(base_row(me ^ r, width) + h * rows, rows), rows)
                for m in range(3):
                    row = (3 * i + m) * rows
                    out[row : row + rows, :] = g_s[m, place, :]
        place = pl.ds(pl.multiple_of(base_row(me, width) + h * rows, rows), rows)
        for m in range(3):
            w0_refs[h][m * rows : (m + 1) * rows, :] = w[m, place, :]


def first_grads(me, k, v, r, init):
    _, tok, width = k.shape
    rows = 3 * width // 2 // CHUNKS
    square = pltpu.VMEM((tok, width), bf16)
    weights = pltpu.VMEM((3, width, width), bf16)
    return pl.pallas_call(
        first_grads_kernel,
        grid=(1,),
        out_shape=[jax.ShapeDtypeStruct((rows, width), bf16)] * (2 * CHUNKS)
        + [jax.ShapeDtypeStruct((rows // 4, width), bf16)] * CHUNKS,
        in_specs=[SMEM, HBM, HBM, pl.BlockSpec((None, 1, tok), lambda i: (0, 0, 0)), HBM],
        out_specs=[VMEM] * (3 * CHUNKS),
        scratch_shapes=[square, square, weights, square, square, square, square, weights, pltpu.SemaphoreType.DMA((5,))],
        compiler_params=params(),
        name="first_grads",
    )(me, in_hbm(k), in_hbm(v), in_hbm(r), in_hbm(init))


def next_grads_kernel(n_w, me_ref, own_hbm, other_hbm, *refs):
    w_refs, out_refs, w_out = refs[:n_w], refs[n_w : n_w + 4 * CHUNKS], refs[n_w + 4 * CHUNKS]
    tok_s, da_s, db_s, hid_s, g_s, w, sems = refs[n_w + 4 * CHUNKS + 1 :]
    loads = [
        [pltpu.make_async_copy(ref.at[j], tok_s.at[i, j], sems.at[2 * i + j]) for j in range(2)]
        for i, ref in enumerate((own_hbm, other_hbm))
    ]
    for pair in loads:
        for load in pair:
            load.start()
    me = me_ref[0]
    assemble(me, w_refs, w)
    keep_w = pltpu.make_async_copy(w, w_out, sems.at[4])
    tok, width = tok_s.shape[2:]
    half = width // 2
    for i, pair in enumerate(loads):

        def ready(name, pair=pair):
            if name != "linear":
                pair[name == "output"].wait()

        token_grads(tok_s.at[i, 0], tok_s.at[i, 1], w, da_s, db_s, hid_s, i * tok, ready)
    keep_w.start()
    mine = pl.ds(pl.multiple_of((me % 2) * half, half), half)
    over_tokens = ((0,), (0,))
    spans = ((0, slice(0, tok)), (1, slice(tok, 2 * tok)))
    for m, d_s in ((0, da_s), (1, db_s)):
        g_s[m] = sum(dot(tok_s[i, 0, :, mine], d_s[span, :], over_tokens) for i, span in spans).astype(bf16)
    g_s[2] = sum(dot(hid_s[span, mine], tok_s[i, 1], over_tokens) for i, span in spans).astype(bf16)
    rows = width // SHARDS // CHUNKS
    for h in range(CHUNKS):
        for i, r in enumerate((0, 2, 4, 6)):
            place = pl.ds(pl.multiple_of((me ^ r) // 2 * (rows * CHUNKS) + h * rows, rows), rows)
            for m in range(3):
                out_refs[4 * h + i][m * rows : (m + 1) * rows, :] = g_s[m, place, :]
    keep_w.wait()


def next_grads(me, own, other, w):
    _, tok, width = own.shape
    rows = 3 * width // SHARDS // CHUNKS
    return pl.pallas_call(
        functools.partial(next_grads_kernel, len(w)),
        out_shape=[jax.ShapeDtypeStruct((rows, width), bf16)] * (4 * CHUNKS) + [pltpu.HBM((3, width, width), bf16)],
        in_specs=[SMEM, HBM, HBM] + [VMEM] * len(w),
        out_specs=[VMEM] * (4 * CHUNKS) + [HBM],
        scratch_shapes=[pltpu.VMEM((2, 2, tok, width), bf16)]
        + [pltpu.VMEM((2 * tok, width), bf16)] * 3
        + [pltpu.VMEM((3, width // 2, width), bf16), pltpu.VMEM((3, width, width), bf16), pltpu.SemaphoreType.DMA((5,))],
        compiler_params=params(),
        name="next_grads",
    )(me, in_hbm(own), in_hbm(other), *w)


def join_kernel(*refs):
    rows = refs[0].shape[0]
    for i, ref in enumerate(refs[:-1]):
        refs[-1][i * rows : (i + 1) * rows, :] = ref[...]


def join(pieces):
    rows, width = pieces[0].shape
    return pl.pallas_call(
        join_kernel,
        out_shape=jax.ShapeDtypeStruct((len(pieces) * rows, width), bf16),
        in_specs=[VMEM] * len(pieces),
        out_specs=VMEM,
        compiler_params=params(),
        name="join",
    )(*pieces)


def update_kernel(keep, p_ref, q_ref, w_ref, *refs):
    moment = p_ref[...].astype(f32) + q_ref[...].astype(f32)
    weights = w_ref[...].astype(f32)
    n_out = 3 if keep else 1
    if len(refs) > n_out:
        moment = momentum_beta * refs[0][...] + moment
    outs = refs[-n_out:]
    unit = moment * lax.rsqrt(jnp.mean(moment * moment, axis=-1, keepdims=True) + 1e-05)
    moved = weights + step_size * unit
    old_sq = jnp.mean(weights * weights, axis=-1, keepdims=True) + 1e-06
    new_sq = jnp.mean(moved * moved, axis=-1, keepdims=True) + 1e-06
    weights = moved * jnp.sqrt(old_sq / new_sq)
    outs[0][...] = weights.astype(bf16)
    if keep:
        outs[1][...] = weights
        outs[2][...] = moment


def update(p, q, state, keep):
    out = [jax.ShapeDtypeStruct(p.shape, bf16)] + [jax.ShapeDtypeStruct(p.shape, f32)] * (2 if keep else 0)
    got = pl.pallas_call(
        functools.partial(update_kernel, keep),
        out_shape=out,
        in_specs=[VMEM] * (2 + len(state)),
        out_specs=[VMEM] * len(out),
        compiler_params=params(),
        name="update",
    )(p, q, *state)
    return got[0], got[1:]


def apply_kernel(n_w, me_ref, q_ref, *refs):
    w_refs, out = refs[:n_w], refs[n_w]
    if n_w == 1:
        w = w_refs[0]
    else:
        w = refs[n_w + 1]
        assemble(me_ref[0], w_refs, w)
    tok = q_ref.shape[0]
    chunk = min(tok, 512)
    for t in range(0, tok, chunk):
        span = slice(t, t + chunk)
        q = q_ref[span, :]
        a = dot(q, w[0])
        b = dot(q, w[1])
        hid = (a * sigmoid(a) * b).astype(bf16)
        out[span, :] = dot(hid, w[2]).astype(bf16)


def fast_apply(me, q, block, w):
    _, tok, width = q.shape
    whole = pl.BlockSpec((3, width, width), lambda i: (0, 0, 0))
    return pl.pallas_call(
        functools.partial(apply_kernel, len(w)),
        grid=(1,),
        out_shape=jax.ShapeDtypeStruct((tok, width), bf16),
        in_specs=[SMEM, pl.BlockSpec((None, tok, width), lambda i: (block, 0, 0))] + ([whole] if len(w) == 1 else [VMEM] * len(w)),
        out_specs=VMEM,
        scratch_shapes=[pltpu.VMEM((3, width, width), bf16)] if len(w) > 1 else [],
        compiler_params=params(),
        name="apply",
    )(me, q, *w)


def project_own_kernel(o_ref, proj_ref, out):
    out[...] = dot(o_ref[...], proj_ref[...])


def project_own(o, proj):
    return pl.pallas_call(
        project_own_kernel,
        out_shape=jax.ShapeDtypeStruct((o.shape[0], proj.shape[1]), f32),
        in_specs=[VMEM] * 2,
        out_specs=VMEM,
        compiler_params=params(),
        name="project_own",
    )(o, proj)


def project_kernel(sum_ref, o_ref, proj_ref, *refs):
    refs[-1][...] = (sum_ref[...] + dot(o_ref[...], proj_ref[...])).astype(bf16)


def project(block, blocks, own, o_other, proj_other, into):
    tok, width = o_other.shape
    cols = proj_other.shape[1]
    args = [own, o_other, proj_other]
    specs = [pl.BlockSpec(x.shape, lambda i: (0, 0)) for x in args]
    aliases = {}
    if into is not None:
        args.append(into)
        specs.append(pl.BlockSpec(memory_space=pl.ANY))
        aliases = {3: 0}
    return pl.pallas_call(
        project_kernel,
        grid=(1,),
        out_shape=jax.ShapeDtypeStruct((blocks, tok, cols), bf16),
        in_specs=specs,
        out_specs=pl.BlockSpec((None, tok, cols), lambda i: (block, 0, 0)),
        input_output_aliases=aliases,
        compiler_params=params(),
        name="project",
    )(*args)


SHARDS = 8
CHUNKS = 2
O = {'join': (0, 0), 't01': 0, 'flows': (0, 1, 2), 'aflows': (0, 1, 2), 'p0_after_t1': 0, 'p01': (0, 0), 'u01': (0, 0), 'tokdone': '', 'tok': 'p0', 'j01': (0, 0), 'app': 'wb', 'res': 'me', 's2': ((0, 0), (0, 0)), 'A': ((0, 0), (0, 0)), 'jf': (0, 0)}
FLOWS = ((1, 2), (2, 4), (3, 6))


def swap_low_bits(i):
    return (i & ~3) | ((i & 1) << 1) | ((i >> 1) & 1)


def together(*values):
    return lax.optimization_barrier(values)


def after(x, *others):
    return together(x, *others)[0]


def solution(mesh):
    ctx, heads = mesh.shape["ctx"], mesh.shape["head"]
    assert ctx & (ctx - 1) == 0 and ctx >= SHARDS and heads == 2

    def swap(x, bits):
        pairs = [(2 * i, 2 * (i ^ bits)) for i in range(ctx)]
        pairs += [(2 * i + 1, 2 * (i ^ swap_low_bits(bits)) + 1) for i in range(ctx)]
        return lax.ppermute(x, ("ctx", "head"), pairs)

    def swap_head(x):
        return lax.ppermute(x, "head", [(0, 1), (1, 0)])

    def add(x, y):
        return x.astype(f32) + y.astype(f32)

    def reduce_half(received, keep):
        total = add(keep, received)
        n = total.shape[0] // 4
        return [total[i * n : (i + 1) * n] for i in range(4)]

    def reduce_pieces(pieces, received):
        p = sum((x.astype(f32) for x in received), pieces[0].astype(f32)).astype(bf16)
        bit = SHARDS
        while bit < ctx // 2:
            p = add(p, swap(p, bit)).astype(bf16)
            bit *= 2
        return p

    def last_exchange(p):
        return swap(p, ctx // 2) if ctx > SHARDS else jnp.zeros_like(p)

    def on_device(queries, key_vectors, value_vectors, token_rates, fast_init, out_proj):
        blocks, tok, _, width = queries.shape
        flat = lambda x: x.reshape(blocks, tok, width)
        q, k, v = flat(queries), flat(key_vectors), flat(value_vectors)
        r = token_rates.reshape(blocks, 1, tok)
        init, proj_all = fast_init[0], out_proj[0]
        head = lax.axis_index("head")
        label = (lax.axis_index("ctx") % SHARDS).astype(jnp.int32)
        me = jnp.where(head == 0, label, swap_low_bits(label)).reshape(1)
        half = proj_all.shape[1] // heads
        proj = lax.dynamic_slice_in_dim(proj_all, head * half, half, 1)
        tokens = None
        if blocks > 1:
            dy = (r[1, 0][:, None] * v[1].astype(f32)).astype(bf16)
            tokens = jnp.stack([k[1], dy])
        proj_other = swap_head(lax.dynamic_slice_in_dim(proj_all, (1 - head) * half, half, 1))

        def finish(c, me, w, into):
            o = fast_apply(me, q, c, w)
            return project(c, blocks, project_own(o, proj), swap_head(o), proj_other, into)

        result = None
        for c in range(blocks):
            last = c + 1 == blocks
            jn = join if O["join"][c] else jnp.concatenate
            if c == 0:
                grads = first_grads(me, k, v, r, init)
                state = [[w0] for w0 in grads[2 * CHUNKS :]]
                received = [swap(grads[2 * h], 1) for h in range(CHUNKS)]
                pieces = []
                for h in range(CHUNKS):
                    got = after(received[h], pieces[-1][0]) if h and O["t01"] else received[h]
                    pieces.append(reduce_half(got, grads[2 * h + 1]))
            else:
                grads = next_grads(me, tokens, tokens_other, w)
                pieces = [grads[4 * h : 4 * h + 4] for h in range(CHUNKS)]
            flows = [FLOWS[i] for i in O["flows"]]
            received = []
            for h in range(CHUNKS):
                ps = pieces[h]
                if O["s2"][c][h]:
                    got = swap(jnp.concatenate([ps[1].astype(bf16), ps[3].astype(bf16)]), 2)
                    n = got.shape[0] // 2
                    mine, send = add(ps[0], got[:n]), add(ps[2], got[n:]).astype(bf16)
                    pieces[h] = [mine]
                    received.append([swap(send, 4)])
                else:
                    received.append([swap(ps[i].astype(bf16), bits) for i, bits in flows])
            sums, near = [], []
            if c == 0 and O["p0_after_t1"]:
                received[0][0] = after(received[0][0], pieces[1][0])
            for h in range(CHUNKS):
                if h and O["p01"][c]:
                    received[h][0] = after(received[h][0], sums[-1])
                sums.append(reduce_pieces(pieces[h], received[h]))
            others = [last_exchange(p) for p in sums]
            for h in range(CHUNKS):
                if h:
                    extra = []
                    if O["u01"][c]: extra.append(near[-1][0])
                    if not last and O["tokdone"] == "q1": extra.append(tokens_other)
                    if extra: others[h] = after(others[h], *extra)
                wb, state[h] = update(sums[h], others[h], state[h], not last)
                if O["A"][c][h]:
                    z = swap(wb, 4)
                    g = swap(jnp.concatenate([wb, z]), 2)
                    n = wb.shape[0]
                    near.append([wb, g[:n], z, g[n:]])
                else:
                    got = {FLOWS[i][1]: swap(wb, FLOWS[i][1]) for i in O["aflows"]}
                    near.append([wb] + [got[bits] for bits in (2, 4, 6)])
                if not last and h == 0:
                    dep = {"grads": grads[0], "p0": sums[0], "t1": pieces[1][0], "t0": pieces[0][0], "p1": sums[1], "wb0": wb, "keep": grads[1]}[O["tok"]]
                    tokens_other = swap(after(tokens, dep), 1)
            joined, far = [], []
            for h in range(CHUNKS):
                ps = list(near[h])
                if h and O["j01"][c]: ps[0] = after(ps[0], joined[-1])
                if h and not last and O["tokdone"] == "j1": ps[0] = after(ps[0], tokens_other)
                if h and O["jf"][c]: ps[0] = after(ps[0], far[0])
                joined.append(jn(ps))
                far.append(swap(joined[-1], 1))
            if c > 0:
                deps = {"w1": [near[1][0]], "w0": [near[0][0]], "z": near[0][1:] + near[1][1:], "z1": near[1][1:], "z0": near[0][1:], "j": joined, "f0": far[:1], "f1": far[1:], "n": [], "wb": [near[1][0], near[0][0]], "p": sums}[O["app"]]
                me_late = after(me, *deps) if deps else me
                result = finish(c - 1, me_late, grads[4 * CHUNKS :], result)
                if O["res"] == "me":
                    me, result = together(me, result)
            w = [x for h in range(CHUNKS) for x in (*near[h], far[h])]
        return finish(blocks - 1, me, w, result)

    placed = (
        P(None, "ctx", "head", None),
        P(None, "ctx", "head", None),
        P(None, "ctx", "head", None),
        P(None, "ctx", "head"),
        P("head", None, None, None),
        P("head", None, None),
    )
    return jax.shard_map(on_device, mesh=mesh, in_specs=placed, out_specs=P(None, "ctx", "head"), check_vma=False)
```

```python
import functools

import jax
import jax.numpy as jnp
from jax import lax
from jax.experimental import pallas as pl
from jax.experimental.pallas import tpu as pltpu
from jax.sharding import PartitionSpec as P

momentum_beta = 0.9
step_size = 0.03
f32 = jnp.float32
bf16 = jnp.bfloat16
VMEM = pl.BlockSpec(memory_space=pltpu.VMEM)
HBM = pl.BlockSpec(memory_space=pltpu.HBM)
SMEM = pl.BlockSpec(memory_space=pltpu.SMEM)


def params(mib=24):
    return pltpu.CompilerParams(vmem_limit_bytes=mib * 2**20)


def in_hbm(x):
    return pltpu.with_memory_space_constraint(x, pltpu.HBM)


def dot(x, y, contract=((1,), (0,))):
    return lax.dot_general(x, y, (contract, ((), ())), preferred_element_type=f32)


def sigmoid(x):
    return 0.5 * jnp.tanh(0.5 * x) + 0.5


def base_row(owner, width):
    return ((owner % 2) * (SHARDS // 2) + owner // 2) * (width // SHARDS)


def pieces_of(chunk, mine):
    found = [(i, 0, r) for i, r in enumerate((0, 2, 4, 6))]
    return found + [(4, i * mine, r) for i, r in enumerate((1, 3, 5, 7))]


def assemble(me, refs, full):
    width = full.shape[1]
    chunks = len(refs) // 5
    rows = width // SHARDS // chunks
    for h in range(chunks):
        for i, first, r in pieces_of(h, 3 * rows):
            ref = refs[5 * h + i]
            place = pl.ds(pl.multiple_of(base_row(me ^ r, width) + h * rows, rows), rows)
            for m in range(3):
                full[m, place, :] = ref[first + m * rows : first + (m + 1) * rows, :]


def token_grads(k, dy, w, da_s, db_s, hid_s, at, ready=lambda name: None):
    tok = k.shape[0]
    chunk = min(tok, 512)
    for t in range(0, tok, chunk):
        rows, span = slice(t, t + chunk), slice(at + t, at + t + chunk)
        if t == 0:
            ready("gate")
        a = dot(k[rows, :], w[0])
        if t == 0:
            ready("linear")
        b = dot(k[rows, :], w[1])
        sig = sigmoid(a)
        silu = a * sig
        hid_s[span, :] = (silu * b).astype(bf16)
        if t == 0:
            ready("output")
        dh = dot(dy[rows, :], w[2], ((1,), (1,)))
        da_s[span, :] = (dh * (b * (sig + silu * (1.0 - sig)))).astype(bf16)
        db_s[span, :] = (dh * silu).astype(bf16)


def first_grads_kernel(me_ref, k_hbm, v_hbm, r_hbm, w_hbm, *refs):
    out_refs, w0_refs = refs[: 2 * CHUNKS], refs[2 * CHUNKS : 3 * CHUNKS]
    k_s, v_s, w, da_s, db_s, hid_s, dy_s, g_s, r_s, sems = refs[3 * CHUNKS :]
    copies = [pltpu.make_async_copy(k_hbm.at[0], k_s, sems.at[0]), pltpu.make_async_copy(v_hbm.at[0], v_s, sems.at[1])]
    copies += [pltpu.make_async_copy(w_hbm.at[m], w.at[m], sems.at[2 + m]) for m in range(3)]
    copies.append(pltpu.make_async_copy(r_hbm.at[0], r_s, sems.at[5]))
    for i in (0, 2, 3, 5, 1, 4):
        copies[i].start()
    me = me_ref[0]
    tok, width = k_s.shape

    def ready(name):
        for i in {"gate": (0, 2), "linear": (3,), "output": (5, 1, 4)}[name]:
            copies[i].wait()
        if name == "output":
            rate_col = jnp.broadcast_to(r_s[...], (8, tok)).T[:, :1]
            dy_s[...] = (rate_col * v_s[...].astype(f32)).astype(bf16)

    token_grads(k_s, dy_s, w, da_s, db_s, hid_s, 0, ready)
    over_tokens = ((0,), (0,))
    g_s[0] = dot(k_s[...], da_s[...], over_tokens).astype(bf16)
    g_s[1] = dot(k_s[...], db_s[...], over_tokens).astype(bf16)
    g_s[2] = dot(hid_s[...], dy_s[...], over_tokens).astype(bf16)
    rows = width // SHARDS // CHUNKS
    for h in range(CHUNKS):
        for out, relative in ((out_refs[2 * h], (1, 3, 5, 7)), (out_refs[2 * h + 1], (0, 2, 4, 6))):
            for i, r in enumerate(relative):
                place = pl.ds(pl.multiple_of(base_row(me ^ r, width) + h * rows, rows), rows)
                for m in range(3):
                    row = (3 * i + m) * rows
                    out[row : row + rows, :] = g_s[m, place, :]
        place = pl.ds(pl.multiple_of(base_row(me, width) + h * rows, rows), rows)
        for m in range(3):
            w0_refs[h][m * rows : (m + 1) * rows, :] = w[m, place, :]


def first_grads(me, k, v, r, init):
    _, tok, width = k.shape
    rows = 3 * width // 2 // CHUNKS
    square = pltpu.VMEM((tok, width), bf16)
    weights = pltpu.VMEM((3, width, width), bf16)
    return pl.pallas_call(
        first_grads_kernel,
        out_shape=[jax.ShapeDtypeStruct((rows, width), bf16)] * (2 * CHUNKS)
        + [jax.ShapeDtypeStruct((rows // 4, width), bf16)] * CHUNKS,
        in_specs=[SMEM] + [HBM] * 4,
        out_specs=[VMEM] * (3 * CHUNKS),
        scratch_shapes=[square, square, weights, square, square, square, square, weights, pltpu.VMEM((1, tok), f32), pltpu.SemaphoreType.DMA((6,))],
        compiler_params=params(),
        name="first_grads",
    )(me, in_hbm(k), in_hbm(v), in_hbm(r), in_hbm(init))


def next_grads_kernel(n_w, me_ref, own_hbm, other_hbm, *refs):
    w_refs, out_refs, w_out = refs[:n_w], refs[n_w : n_w + 4 * CHUNKS], refs[n_w + 4 * CHUNKS]
    tok_s, da_s, db_s, hid_s, g_s, w, sems = refs[n_w + 4 * CHUNKS + 1 :]
    loads = [
        [pltpu.make_async_copy(ref.at[j], tok_s.at[i, j], sems.at[2 * i + j]) for j in range(2)]
        for i, ref in enumerate((own_hbm, other_hbm))
    ]
    for pair in loads:
        for load in pair:
            load.start()
    me = me_ref[0]
    assemble(me, w_refs, w)
    keep_w = pltpu.make_async_copy(w, w_out, sems.at[4])
    tok, width = tok_s.shape[2:]
    half = width // 2
    for i, pair in enumerate(loads):

        def ready(name, pair=pair):
            if name != "linear":
                pair[name == "output"].wait()

        token_grads(tok_s.at[i, 0], tok_s.at[i, 1], w, da_s, db_s, hid_s, i * tok, ready)
    keep_w.start()
    mine = pl.ds(pl.multiple_of((me % 2) * half, half), half)
    over_tokens = ((0,), (0,))
    spans = ((0, slice(0, tok)), (1, slice(tok, 2 * tok)))
    for m, d_s in ((0, da_s), (1, db_s)):
        g_s[m] = sum(dot(tok_s[i, 0, :, mine], d_s[span, :], over_tokens) for i, span in spans).astype(bf16)
    g_s[2] = sum(dot(hid_s[span, mine], tok_s[i, 1], over_tokens) for i, span in spans).astype(bf16)
    rows = width // SHARDS // CHUNKS
    for h in range(CHUNKS):
        for i, r in enumerate((0, 2, 4, 6)):
            place = pl.ds(pl.multiple_of((me ^ r) // 2 * (rows * CHUNKS) + h * rows, rows), rows)
            for m in range(3):
                out_refs[4 * h + i][m * rows : (m + 1) * rows, :] = g_s[m, place, :]
    keep_w.wait()


def next_grads(me, own, other, w):
    _, tok, width = own.shape
    rows = 3 * width // SHARDS // CHUNKS
    return pl.pallas_call(
        functools.partial(next_grads_kernel, len(w)),
        out_shape=[jax.ShapeDtypeStruct((rows, width), bf16)] * (4 * CHUNKS) + [pltpu.HBM((3, width, width), bf16)],
        in_specs=[SMEM, HBM, HBM] + [VMEM] * len(w),
        out_specs=[VMEM] * (4 * CHUNKS) + [HBM],
        scratch_shapes=[pltpu.VMEM((2, 2, tok, width), bf16)]
        + [pltpu.VMEM((2 * tok, width), bf16)] * 3
        + [pltpu.VMEM((3, width // 2, width), bf16), pltpu.VMEM((3, width, width), bf16), pltpu.SemaphoreType.DMA((5,))],
        compiler_params=params(),
        name="next_grads",
    )(me, in_hbm(own), in_hbm(other), *w)


def tokens_kernel(k_hbm, v_hbm, r_hbm, out, k_s, v_s, r_s, sems):
    loads = [pltpu.make_async_copy(x.at[1], x_s, sems.at[i]) for i, (x, x_s) in enumerate(((v_hbm, v_s), (r_hbm, r_s), (k_hbm, k_s)))]
    for load in loads:
        load.start()
    tok = v_s.shape[0]
    loads[0].wait()
    loads[1].wait()
    rate_col = jnp.broadcast_to(r_s[...], (8, tok)).T[:, :1]
    v_s[...] = (rate_col * v_s[...].astype(f32)).astype(bf16)
    loads[2].wait()
    stores = [pltpu.make_async_copy(x_s, out.at[i], sems.at[3 + i]) for i, x_s in enumerate((k_s, v_s))]
    for store in stores:
        store.start()
    for store in stores:
        store.wait()


def next_tokens(k, v, r):
    _, tok, width = k.shape
    square = pltpu.VMEM((tok, width), bf16)
    return pl.pallas_call(
        tokens_kernel,
        out_shape=pltpu.HBM((2, tok, width), bf16),
        in_specs=[HBM] * 3,
        out_specs=HBM,
        scratch_shapes=[square, square, pltpu.VMEM((1, tok), f32), pltpu.SemaphoreType.DMA((5,))],
        compiler_params=params(),
        name="next_tokens",
    )(in_hbm(k), in_hbm(v), in_hbm(r))


def update_kernel(keep, p_ref, q_ref, w_ref, *refs):
    moment = p_ref[...].astype(f32) + q_ref[...].astype(f32)
    weights = w_ref[...].astype(f32)
    n_out = 3 if keep else 1
    if len(refs) > n_out:
        moment = momentum_beta * refs[0][...] + moment
    outs = refs[-n_out:]
    unit = moment * lax.rsqrt(jnp.mean(moment * moment, axis=-1, keepdims=True) + 1e-05)
    moved = weights + step_size * unit
    old_sq = jnp.mean(weights * weights, axis=-1, keepdims=True) + 1e-06
    new_sq = jnp.mean(moved * moved, axis=-1, keepdims=True) + 1e-06
    weights = moved * jnp.sqrt(old_sq / new_sq)
    outs[0][...] = weights.astype(bf16)
    if keep:
        outs[1][...] = weights
        outs[2][...] = moment


def update(p, q, state, keep):
    out = [jax.ShapeDtypeStruct(p.shape, bf16)] + [jax.ShapeDtypeStruct(p.shape, f32)] * (2 if keep else 0)
    got = pl.pallas_call(
        functools.partial(update_kernel, keep),
        out_shape=out,
        in_specs=[VMEM] * (2 + len(state)),
        out_specs=[VMEM] * len(out),
        compiler_params=params(),
        name="update",
    )(p, q, *state)
    return got[0], got[1:]


def apply_kernel(n_w, me_ref, q_ref, *refs):
    w_refs, out = refs[:n_w], refs[n_w]
    if n_w == 1:
        w = w_refs[0]
    else:
        w = refs[n_w + 1]
        assemble(me_ref[0], w_refs, w)
    tok = q_ref.shape[0]
    chunk = min(tok, 512)
    for t in range(0, tok, chunk):
        span = slice(t, t + chunk)
        q = q_ref[span, :]
        a = dot(q, w[0])
        b = dot(q, w[1])
        hid = (a * sigmoid(a) * b).astype(bf16)
        out[span, :] = dot(hid, w[2]).astype(bf16)


def fast_apply(me, q, block, w):
    _, tok, width = q.shape
    whole = pl.BlockSpec((3, width, width), lambda i: (0, 0, 0))
    return pl.pallas_call(
        functools.partial(apply_kernel, len(w)),
        grid=(1,),
        out_shape=jax.ShapeDtypeStruct((tok, width), bf16),
        in_specs=[SMEM, pl.BlockSpec((None, tok, width), lambda i: (block, 0, 0))] + ([whole] if len(w) == 1 else [VMEM] * len(w)),
        out_specs=VMEM,
        scratch_shapes=[pltpu.VMEM((3, width, width), bf16)] if len(w) > 1 else [],
        compiler_params=params(),
        name="apply",
    )(me, q, *w)


def project_own_kernel(o_ref, proj_ref, out):
    out[...] = dot(o_ref[...], proj_ref[...])


def project_own(o, proj):
    return pl.pallas_call(
        project_own_kernel,
        out_shape=jax.ShapeDtypeStruct((o.shape[0], proj.shape[1]), f32),
        in_specs=[VMEM] * 2,
        out_specs=VMEM,
        compiler_params=params(),
        name="project_own",
    )(o, proj)


def project_kernel(block, sum_ref, o_ref, proj_ref, *refs):
    out, (out_s, sems) = refs[-3], refs[-2:]
    rows = o_ref.shape[0] // 4
    stores = []
    for i in range(4):
        span = slice(i * rows, (i + 1) * rows)
        out_s[span, :] = (sum_ref[span, :] + dot(o_ref[span, :], proj_ref[...])).astype(bf16)
        stores.append(pltpu.make_async_copy(out_s.at[span, :], out.at[block, span, :], sems.at[i]))
        stores[-1].start()
    for store in stores:
        store.wait()


def project(block, blocks, own, o_other, proj_other, into):
    tok, cols = own.shape
    args = [own, o_other, proj_other] + ([] if into is None else [into])
    return pl.pallas_call(
        functools.partial(project_kernel, block),
        out_shape=jax.ShapeDtypeStruct((blocks, tok, cols), bf16),
        in_specs=[VMEM] * 3 + [pl.BlockSpec(memory_space=pl.ANY)] * (len(args) - 3),
        out_specs=pl.BlockSpec(memory_space=pl.ANY),
        scratch_shapes=[pltpu.VMEM((tok, cols), bf16), pltpu.SemaphoreType.DMA((4,))],
        input_output_aliases={} if into is None else {3: 0},
        compiler_params=params(),
        name="project",
    )(*args)


SHARDS = 8
CHUNKS = 2
FLOWS = ((1, 2), (2, 4), (3, 6))


def swap_low_bits(i):
    return (i & ~3) | ((i & 1) << 1) | ((i >> 1) & 1)


def together(*values):
    return lax.optimization_barrier(values)


def after(x, *others):
    return together(x, *others)[0]


def solution(mesh):
    ctx, heads = mesh.shape["ctx"], mesh.shape["head"]
    assert ctx & (ctx - 1) == 0 and ctx >= SHARDS and heads == 2

    def swap(x, bits):
        pairs = [(2 * i, 2 * (i ^ bits)) for i in range(ctx)]
        pairs += [(2 * i + 1, 2 * (i ^ swap_low_bits(bits)) + 1) for i in range(ctx)]
        return lax.ppermute(x, ("ctx", "head"), pairs)

    def swap_head(x):
        return lax.ppermute(x, "head", [(0, 1), (1, 0)])

    def add(x, y):
        return x.astype(f32) + y.astype(f32)

    def reduce_half(received, keep):
        total = add(keep, received)
        n = total.shape[0] // 4
        return [total[i * n : (i + 1) * n] for i in range(4)]

    def reduce_pieces(pieces, received):
        p = sum((x.astype(f32) for x in received), pieces[0].astype(f32)).astype(bf16)
        bit = SHARDS
        while bit < ctx // 2:
            p = add(p, swap(p, bit)).astype(bf16)
            bit *= 2
        return p

    def last_exchange(p):
        return swap(p, ctx // 2) if ctx > SHARDS else jnp.zeros_like(p)

    def on_device(queries, key_vectors, value_vectors, token_rates, fast_init, out_proj):
        blocks, tok, _, width = queries.shape
        assert blocks == 2
        flat = lambda x: x.reshape(blocks, tok, width)
        q, k, v = flat(queries), flat(key_vectors), flat(value_vectors)
        r = token_rates.reshape(blocks, 1, tok)
        init, proj_all = fast_init[0], out_proj[0]
        head = lax.axis_index("head")
        label = (lax.axis_index("ctx") % SHARDS).astype(jnp.int32)
        me = jnp.where(head == 0, label, swap_low_bits(label)).reshape(1)
        half = proj_all.shape[1] // heads
        proj = lax.dynamic_slice_in_dim(proj_all, head * half, half, 1)
        proj_other = swap_head(lax.dynamic_slice_in_dim(proj_all, (1 - head) * half, half, 1))

        def finish(c, me, w, into):
            o = fast_apply(me, q, c, w)
            return project(c, blocks, project_own(o, proj), swap_head(o), proj_other, into)

        result = None
        for c in range(blocks):
            last = c + 1 == blocks
            if c == 0:
                grads = first_grads(me, k, v, r, init)
                state = [[w0] for w0 in grads[2 * CHUNKS :]]
                tokens = next_tokens(*together(k, v, r, grads[0])[:3])
                received = [swap(grads[2 * h], 1) for h in range(CHUNKS)]
                pieces = [reduce_half(received[h], grads[2 * h + 1]) for h in range(CHUNKS)]
            else:
                grads = next_grads(me, tokens, tokens_other, w)
                pieces = [grads[4 * h : 4 * h + 4] for h in range(CHUNKS)]
            received = [[swap(pieces[h][i].astype(bf16), bits) for i, bits in FLOWS] for h in range(CHUNKS)]
            sums = [reduce_pieces(pieces[h], received[h]) for h in range(CHUNKS)]
            others = [last_exchange(p) for p in sums]
            near = []
            for h in range(CHUNKS):
                wb, state[h] = update(sums[h], others[h], state[h], not last)
                got = {bits: swap(wb, bits) for _, bits in FLOWS}
                near.append([wb] + [got[bits] for bits in (2, 4, 6)])
                if not last and h == 0:
                    tokens_other = swap(after(tokens, sums[0]), 1)
            joined, far = [], []
            for h in range(CHUNKS):
                parts = list(near[h])
                if h and last:
                    parts[0] = after(parts[0], joined[-1])
                joined.append(jnp.concatenate(parts))
                far.append(swap(joined[-1], 1))
            if c > 0:
                me_late = after(me, near[1][0])
                result = finish(c - 1, me_late, grads[4 * CHUNKS :], result)
                me, result = together(me, result)
            w = [x for h in range(CHUNKS) for x in (*near[h], far[h])]
        return finish(blocks - 1, me, w, result)

    placed = (
        P(None, "ctx", "head", None),
        P(None, "ctx", "head", None),
        P(None, "ctx", "head", None),
        P(None, "ctx", "head"),
        P("head", None, None, None),
        P("head", None, None),
    )
    return jax.shard_map(on_device, mesh=mesh, in_specs=placed, out_specs=P(None, "ctx", "head"), check_vma=False)
```

```python
import functools

import jax
import jax.numpy as jnp
from jax import lax
from jax.experimental import pallas as pl
from jax.experimental.pallas import tpu as pltpu
from jax.sharding import PartitionSpec as P

momentum_beta = 0.9
step_size = 0.03
f32 = jnp.float32
bf16 = jnp.bfloat16
VMEM = pl.BlockSpec(memory_space=pltpu.VMEM)
HBM = pl.BlockSpec(memory_space=pltpu.HBM)
SMEM = pl.BlockSpec(memory_space=pltpu.SMEM)


def params(mib=24):
    return pltpu.CompilerParams(vmem_limit_bytes=mib * 2**20)


def in_hbm(x):
    return pltpu.with_memory_space_constraint(x, pltpu.HBM)


def dot(x, y, contract=((1,), (0,))):
    return lax.dot_general(x, y, (contract, ((), ())), preferred_element_type=f32)


def sigmoid(x):
    return 0.5 * jnp.tanh(0.5 * x) + 0.5


def base_row(owner, width):
    return ((owner % 2) * (SHARDS // 2) + owner // 2) * (width // SHARDS)


def pieces_of(chunk, mine):
    found = [(i, 0, r) for i, r in enumerate((0, 2, 4, 6))]
    return found + [(4, i * mine, r) for i, r in enumerate((1, 3, 5, 7))]


def assemble(me, refs, full):
    width = full.shape[1]
    chunks = len(refs) // 5
    rows = width // SHARDS // chunks
    for h in range(chunks):
        for i, first, r in pieces_of(h, 3 * rows):
            ref = refs[5 * h + i]
            place = pl.ds(pl.multiple_of(base_row(me ^ r, width) + h * rows, rows), rows)
            for m in range(3):
                full[m, place, :] = ref[first + m * rows : first + (m + 1) * rows, :]


def token_grads(k, dy, w, da_s, db_s, hid_s, at, ready=lambda name: None):
    tok = k.shape[0]
    chunk = min(tok, 512)
    for t in range(0, tok, chunk):
        rows, span = slice(t, t + chunk), slice(at + t, at + t + chunk)
        if t == 0:
            ready("gate")
        a = dot(k[rows, :], w[0])
        if t == 0:
            ready("linear")
        b = dot(k[rows, :], w[1])
        sig = sigmoid(a)
        silu = a * sig
        hid_s[span, :] = (silu * b).astype(bf16)
        if t == 0:
            ready("output")
        dh = dot(dy[rows, :], w[2], ((1,), (1,)))
        da_s[span, :] = (dh * (b * (sig + silu * (1.0 - sig)))).astype(bf16)
        db_s[span, :] = (dh * silu).astype(bf16)


def first_grads_kernel(me_ref, k_hbm, v_hbm, r_hbm, w_hbm, *refs):
    out_refs, w0_refs = refs[: 2 * CHUNKS], refs[2 * CHUNKS : 3 * CHUNKS]
    k_s, v_s, w, da_s, db_s, hid_s, dy_s, g_s, r_s, sems = refs[3 * CHUNKS :]
    copies = [pltpu.make_async_copy(k_hbm.at[0], k_s, sems.at[0]), pltpu.make_async_copy(v_hbm.at[0], v_s, sems.at[1])]
    copies += [pltpu.make_async_copy(w_hbm.at[m], w.at[m], sems.at[2 + m]) for m in range(3)]
    copies.append(pltpu.make_async_copy(r_hbm.at[0], r_s, sems.at[5]))
    for i in (0, 2, 3, 5, 1, 4):
        copies[i].start()
    me = me_ref[0]
    tok, width = k_s.shape

    def ready(name):
        for i in {"gate": (0, 2), "linear": (3,), "output": (5, 1, 4)}[name]:
            copies[i].wait()
        if name == "output":
            rate_col = jnp.broadcast_to(r_s[...], (8, tok)).T[:, :1]
            dy_s[...] = (rate_col * v_s[...].astype(f32)).astype(bf16)

    token_grads(k_s, dy_s, w, da_s, db_s, hid_s, 0, ready)
    over_tokens = ((0,), (0,))
    g_s[0] = dot(k_s[...], da_s[...], over_tokens).astype(bf16)
    g_s[1] = dot(k_s[...], db_s[...], over_tokens).astype(bf16)
    g_s[2] = dot(hid_s[...], dy_s[...], over_tokens).astype(bf16)
    rows = width // SHARDS // CHUNKS
    for h in range(CHUNKS):
        for out, relative in ((out_refs[2 * h], (1, 3, 5, 7)), (out_refs[2 * h + 1], (0, 2, 4, 6))):
            for i, r in enumerate(relative):
                place = pl.ds(pl.multiple_of(base_row(me ^ r, width) + h * rows, rows), rows)
                for m in range(3):
                    row = (3 * i + m) * rows
                    out[row : row + rows, :] = g_s[m, place, :]
        place = pl.ds(pl.multiple_of(base_row(me, width) + h * rows, rows), rows)
        for m in range(3):
            w0_refs[h][m * rows : (m + 1) * rows, :] = w[m, place, :]


def first_grads(me, k, v, r, init):
    _, tok, width = k.shape
    rows = 3 * width // 2 // CHUNKS
    square = pltpu.VMEM((tok, width), bf16)
    weights = pltpu.VMEM((3, width, width), bf16)
    return pl.pallas_call(
        first_grads_kernel,
        out_shape=[jax.ShapeDtypeStruct((rows, width), bf16)] * (2 * CHUNKS)
        + [jax.ShapeDtypeStruct((rows // 4, width), bf16)] * CHUNKS,
        in_specs=[SMEM] + [HBM] * 4,
        out_specs=[VMEM] * (3 * CHUNKS),
        scratch_shapes=[square, square, weights, square, square, square, square, weights, pltpu.VMEM((1, tok), f32), pltpu.SemaphoreType.DMA((6,))],
        compiler_params=params(),
        name="first_grads",
    )(me, in_hbm(k), in_hbm(v), in_hbm(r), in_hbm(init))


def next_grads_kernel(n_w, me_ref, own_hbm, other_hbm, *refs):
    w_refs, out_refs, w_out = refs[:n_w], refs[n_w : n_w + 4 * CHUNKS], refs[n_w + 4 * CHUNKS]
    tok_s, da_s, db_s, hid_s, g_s, w, sems = refs[n_w + 4 * CHUNKS + 1 :]
    loads = [
        [pltpu.make_async_copy(ref.at[j], tok_s.at[j, pl.ds(i * own_hbm.shape[1], own_hbm.shape[1])], sems.at[2 * i + j]) for j in range(2)]
        for i, ref in enumerate((own_hbm, other_hbm))
    ]
    for pair in loads:
        for load in pair:
            load.start()
    me = me_ref[0]
    assemble(me, w_refs, w)
    keep_w = pltpu.make_async_copy(w, w_out, sems.at[4])
    tok, width = own_hbm.shape[1:]
    half = width // 2
    for i, pair in enumerate(loads):

        def ready(name, pair=pair):
            if name != "linear":
                pair[name == "output"].wait()

        token_grads(tok_s.at[0, pl.ds(i * tok, tok)], tok_s.at[1, pl.ds(i * tok, tok)], w, da_s, db_s, hid_s, i * tok, ready)
    keep_w.start()
    mine = pl.ds(pl.multiple_of((me % 2) * half, half), half)
    over_tokens = ((0,), (0,))
    g_s[0] = dot(tok_s[0, :, mine], da_s[...], over_tokens).astype(bf16)
    g_s[1] = dot(tok_s[0, :, mine], db_s[...], over_tokens).astype(bf16)
    g_s[2] = dot(hid_s[:, mine], tok_s[1], over_tokens).astype(bf16)
    rows = width // SHARDS // CHUNKS
    for h in range(CHUNKS):
        for i, r in enumerate((0, 2, 4, 6)):
            place = pl.ds(pl.multiple_of((me ^ r) // 2 * (rows * CHUNKS) + h * rows, rows), rows)
            for m in range(3):
                out_refs[4 * h + i][m * rows : (m + 1) * rows, :] = g_s[m, place, :]
    keep_w.wait()


def next_grads(me, own, other, w):
    _, tok, width = own.shape
    rows = 3 * width // SHARDS // CHUNKS
    return pl.pallas_call(
        functools.partial(next_grads_kernel, len(w)),
        out_shape=[jax.ShapeDtypeStruct((rows, width), bf16)] * (4 * CHUNKS) + [pltpu.HBM((3, width, width), bf16)],
        in_specs=[SMEM, HBM, HBM] + [VMEM] * len(w),
        out_specs=[VMEM] * (4 * CHUNKS) + [HBM],
        scratch_shapes=[pltpu.VMEM((2, 2 * tok, width), bf16)]
        + [pltpu.VMEM((2 * tok, width), bf16)] * 3
        + [pltpu.VMEM((3, width // 2, width), bf16), pltpu.VMEM((3, width, width), bf16), pltpu.SemaphoreType.DMA((5,))],
        compiler_params=params(),
        name="next_grads",
    )(me, in_hbm(own), in_hbm(other), *w)


def tokens_kernel(k_hbm, v_hbm, r_hbm, out, k_s, v_s, r_s, sems):
    loads = [pltpu.make_async_copy(x.at[1], x_s, sems.at[i]) for i, (x, x_s) in enumerate(((v_hbm, v_s), (r_hbm, r_s), (k_hbm, k_s)))]
    for load in loads:
        load.start()
    tok = v_s.shape[0]
    loads[0].wait()
    loads[1].wait()
    rate_col = jnp.broadcast_to(r_s[...], (8, tok)).T[:, :1]
    v_s[...] = (rate_col * v_s[...].astype(f32)).astype(bf16)
    loads[2].wait()
    stores = [pltpu.make_async_copy(x_s, out.at[i], sems.at[3 + i]) for i, x_s in enumerate((k_s, v_s))]
    for store in stores:
        store.start()
    for store in stores:
        store.wait()


def next_tokens(k, v, r):
    _, tok, width = k.shape
    square = pltpu.VMEM((tok, width), bf16)
    return pl.pallas_call(
        tokens_kernel,
        out_shape=pltpu.HBM((2, tok, width), bf16),
        in_specs=[HBM] * 3,
        out_specs=HBM,
        scratch_shapes=[square, square, pltpu.VMEM((1, tok), f32), pltpu.SemaphoreType.DMA((5,))],
        compiler_params=params(),
        name="next_tokens",
    )(in_hbm(k), in_hbm(v), in_hbm(r))


def update_kernel(keep, p_ref, q_ref, w_ref, *refs):
    moment = p_ref[...].astype(f32) + q_ref[...].astype(f32)
    weights = w_ref[...].astype(f32)
    n_out = 3 if keep else 1
    if len(refs) > n_out:
        moment = momentum_beta * refs[0][...] + moment
    outs = refs[-n_out:]
    unit = moment * lax.rsqrt(jnp.mean(moment * moment, axis=-1, keepdims=True) + 1e-05)
    moved = weights + step_size * unit
    old_sq = jnp.mean(weights * weights, axis=-1, keepdims=True) + 1e-06
    new_sq = jnp.mean(moved * moved, axis=-1, keepdims=True) + 1e-06
    weights = moved * jnp.sqrt(old_sq / new_sq)
    outs[0][...] = weights.astype(bf16)
    if keep:
        outs[1][...] = weights
        outs[2][...] = moment


def update(p, q, state, keep):
    out = [jax.ShapeDtypeStruct(p.shape, bf16)] + [jax.ShapeDtypeStruct(p.shape, f32)] * (2 if keep else 0)
    got = pl.pallas_call(
        functools.partial(update_kernel, keep),
        out_shape=out,
        in_specs=[VMEM] * (2 + len(state)),
        out_specs=[VMEM] * len(out),
        compiler_params=params(),
        name="update",
    )(p, q, *state)
    return got[0], got[1:]


def apply_kernel(n_w, me_ref, q_ref, *refs):
    w_refs, out = refs[:n_w], refs[n_w]
    if n_w == 1:
        w = w_refs[0]
    else:
        w = refs[n_w + 1]
        assemble(me_ref[0], w_refs, w)
    tok = q_ref.shape[0]
    chunk = min(tok, 512)
    for t in range(0, tok, chunk):
        span = slice(t, t + chunk)
        q = q_ref[span, :]
        a = dot(q, w[0])
        b = dot(q, w[1])
        hid = (a * sigmoid(a) * b).astype(bf16)
        out[span, :] = dot(hid, w[2]).astype(bf16)


def fast_apply(me, q, block, w):
    _, tok, width = q.shape
    whole = pl.BlockSpec((3, width, width), lambda i: (0, 0, 0))
    return pl.pallas_call(
        functools.partial(apply_kernel, len(w)),
        grid=(1,),
        out_shape=jax.ShapeDtypeStruct((tok, width), bf16),
        in_specs=[SMEM, pl.BlockSpec((None, tok, width), lambda i: (block, 0, 0))] + ([whole] if len(w) == 1 else [VMEM] * len(w)),
        out_specs=VMEM,
        scratch_shapes=[pltpu.VMEM((3, width, width), bf16)] if len(w) > 1 else [],
        compiler_params=params(),
        name="apply",
    )(me, q, *w)


def project_own_kernel(o_ref, proj_ref, out):
    out[...] = dot(o_ref[...], proj_ref[...])


def project_own(o, proj):
    return pl.pallas_call(
        project_own_kernel,
        out_shape=jax.ShapeDtypeStruct((o.shape[0], proj.shape[1]), f32),
        in_specs=[VMEM] * 2,
        out_specs=VMEM,
        compiler_params=params(),
        name="project_own",
    )(o, proj)


def project_kernel(block, sum_ref, o_ref, proj_ref, *refs):
    out, (out_s, sems) = refs[-3], refs[-2:]
    rows = o_ref.shape[0] // 4
    stores = []
    for i in range(4):
        span = slice(i * rows, (i + 1) * rows)
        out_s[span, :] = (sum_ref[span, :] + dot(o_ref[span, :], proj_ref[...])).astype(bf16)
        stores.append(pltpu.make_async_copy(out_s.at[span, :], out.at[block, span, :], sems.at[i]))
        stores[-1].start()
    for store in stores:
        store.wait()


def project(block, blocks, own, o_other, proj_other, into):
    tok, cols = own.shape
    args = [own, o_other, proj_other] + ([] if into is None else [into])
    return pl.pallas_call(
        functools.partial(project_kernel, block),
        out_shape=jax.ShapeDtypeStruct((blocks, tok, cols), bf16),
        in_specs=[VMEM] * 3 + [pl.BlockSpec(memory_space=pl.ANY)] * (len(args) - 3),
        out_specs=pl.BlockSpec(memory_space=pl.ANY),
        scratch_shapes=[pltpu.VMEM((tok, cols), bf16), pltpu.SemaphoreType.DMA((4,))],
        input_output_aliases={} if into is None else {3: 0},
        compiler_params=params(),
        name="project",
    )(*args)


SHARDS = 8
CHUNKS = 2
FLOWS = ((1, 2), (2, 4), (3, 6))


def swap_low_bits(i):
    return (i & ~3) | ((i & 1) << 1) | ((i >> 1) & 1)


def together(*values):
    return lax.optimization_barrier(values)


def after(x, *others):
    return together(x, *others)[0]


def solution(mesh):
    ctx, heads = mesh.shape["ctx"], mesh.shape["head"]
    assert ctx & (ctx - 1) == 0 and ctx >= SHARDS and heads == 2

    def swap(x, bits):
        pairs = [(2 * i, 2 * (i ^ bits)) for i in range(ctx)]
        pairs += [(2 * i + 1, 2 * (i ^ swap_low_bits(bits)) + 1) for i in range(ctx)]
        return lax.ppermute(x, ("ctx", "head"), pairs)

    def swap_head(x):
        return lax.ppermute(x, "head", [(0, 1), (1, 0)])

    def add(x, y):
        return x.astype(f32) + y.astype(f32)

    def reduce_half(received, keep):
        total = add(keep, received)
        n = total.shape[0] // 4
        return [total[i * n : (i + 1) * n] for i in range(4)]

    def reduce_pieces(pieces, received):
        p = sum((x.astype(f32) for x in received), pieces[0].astype(f32)).astype(bf16)
        bit = SHARDS
        while bit < ctx // 2:
            p = add(p, swap(p, bit)).astype(bf16)
            bit *= 2
        return p

    def last_exchange(p):
        return swap(p, ctx // 2) if ctx > SHARDS else jnp.zeros_like(p)

    def on_device(queries, key_vectors, value_vectors, token_rates, fast_init, out_proj):
        blocks, tok, _, width = queries.shape
        assert blocks == 2
        flat = lambda x: x.reshape(blocks, tok, width)
        q, k, v = flat(queries), flat(key_vectors), flat(value_vectors)
        r = token_rates.reshape(blocks, 1, tok)
        init, proj_all = fast_init[0], out_proj[0]
        head = lax.axis_index("head")
        label = (lax.axis_index("ctx") % SHARDS).astype(jnp.int32)
        me = jnp.where(head == 0, label, swap_low_bits(label)).reshape(1)
        half = proj_all.shape[1] // heads
        proj = lax.dynamic_slice_in_dim(proj_all, head * half, half, 1)
        proj_other = swap_head(lax.dynamic_slice_in_dim(proj_all, (1 - head) * half, half, 1))

        def finish(c, me, w, into):
            o = fast_apply(me, q, c, w)
            return project(c, blocks, project_own(o, proj), swap_head(o), proj_other, into)

        result = None
        for c in range(blocks):
            last = c + 1 == blocks
            if c == 0:
                grads = first_grads(me, k, v, r, init)
                state = [[w0] for w0 in grads[2 * CHUNKS :]]
                tokens = next_tokens(*together(k, v, r, grads[0])[:3])
                received = [swap(grads[2 * h], 1) for h in range(CHUNKS)]
                pieces = [reduce_half(received[h], grads[2 * h + 1]) for h in range(CHUNKS)]
            else:
                grads = next_grads(me, tokens, tokens_other, w)
                pieces = [grads[4 * h : 4 * h + 4] for h in range(CHUNKS)]
            received = [[swap(pieces[h][i].astype(bf16), bits) for i, bits in FLOWS] for h in range(CHUNKS)]
            sums = [reduce_pieces(pieces[h], received[h]) for h in range(CHUNKS)]
            others = [last_exchange(p) for p in sums]
            near = []
            for h in range(CHUNKS):
                wb, state[h] = update(sums[h], others[h], state[h], not last)
                got = {bits: swap(wb, bits) for _, bits in FLOWS}
                near.append([wb] + [got[bits] for bits in (2, 4, 6)])
                if not last and h == 0:
                    tokens_other = swap(after(tokens, sums[0]), 1)
            joined, far = [], []
            for h in range(CHUNKS):
                parts = list(near[h])
                if h and last:
                    parts[0] = after(parts[0], joined[-1])
                joined.append(jnp.concatenate(parts))
                far.append(swap(joined[-1], 1))
            if c > 0:
                me_late = after(me, near[1][0])
                result = finish(c - 1, me_late, grads[4 * CHUNKS :], result)
                me, result = together(me, result)
            w = [x for h in range(CHUNKS) for x in (*near[h], far[h])]
        return finish(blocks - 1, me, w, result)

    placed = (
        P(None, "ctx", "head", None),
        P(None, "ctx", "head", None),
        P(None, "ctx", "head", None),
        P(None, "ctx", "head"),
        P("head", None, None, None),
        P("head", None, None),
    )
    return jax.shard_map(on_device, mesh=mesh, in_specs=placed, out_specs=P(None, "ctx", "head"), check_vma=False)
```

```python
import functools

import jax
import jax.numpy as jnp
from jax import lax
from jax.experimental import pallas as pl
from jax.experimental.pallas import tpu as pltpu
from jax.sharding import PartitionSpec as P

momentum_beta = 0.9
step_size = 0.03
f32 = jnp.float32
bf16 = jnp.bfloat16
VMEM = pl.BlockSpec(memory_space=pltpu.VMEM)
HBM = pl.BlockSpec(memory_space=pltpu.HBM)
SMEM = pl.BlockSpec(memory_space=pltpu.SMEM)


def params(mib=24):
    return pltpu.CompilerParams(vmem_limit_bytes=mib * 2**20)


def in_hbm(x):
    return pltpu.with_memory_space_constraint(x, pltpu.HBM)


def dot(x, y, contract=((1,), (0,))):
    return lax.dot_general(x, y, (contract, ((), ())), preferred_element_type=f32)


def sigmoid(x):
    return 0.5 * jnp.tanh(0.5 * x) + 0.5


def base_row(owner, width):
    return ((owner % 2) * (SHARDS // 2) + owner // 2) * (width // SHARDS)


def pieces_of(chunk, mine):
    found = [(i, 0, r) for i, r in enumerate((0, 2, 4, 6))]
    return found + [(4, i * mine, r) for i, r in enumerate((1, 3, 5, 7))]


def assemble(me, refs, full):
    width = full.shape[1]
    chunks = len(refs) // 5
    rows = width // SHARDS // chunks
    for h in range(chunks):
        for i, first, r in pieces_of(h, 3 * rows):
            ref = refs[5 * h + i]
            place = pl.ds(pl.multiple_of(base_row(me ^ r, width) + h * rows, rows), rows)
            for m in range(3):
                full[m, place, :] = ref[first + m * rows : first + (m + 1) * rows, :]


def token_grads(k, dy, w, da_s, db_s, hid_s, at, ready=lambda name: None):
    tok = k.shape[0]
    chunk = min(tok, 512)
    for t in range(0, tok, chunk):
        rows, span = slice(t, t + chunk), slice(at + t, at + t + chunk)
        if t == 0:
            ready("gate")
        a = dot(k[rows, :], w[0])
        if t == 0:
            ready("linear")
        b = dot(k[rows, :], w[1])
        sig = sigmoid(a)
        silu = a * sig
        hid_s[span, :] = (silu * b).astype(bf16)
        if t == 0:
            ready("output")
        dh = dot(dy[rows, :], w[2], ((1,), (1,)))
        da_s[span, :] = (dh * (b * (sig + silu * (1.0 - sig)))).astype(bf16)
        db_s[span, :] = (dh * silu).astype(bf16)


def first_grads_kernel(me_ref, k_hbm, v_hbm, r_hbm, w_hbm, *refs):
    out_refs, w0_refs = refs[: 2 * CHUNKS], refs[2 * CHUNKS : 3 * CHUNKS]
    k_s, v_s, w, da_s, db_s, hid_s, dy_s, g_s, r_s, sems = refs[3 * CHUNKS :]
    copies = [pltpu.make_async_copy(k_hbm.at[0], k_s, sems.at[0]), pltpu.make_async_copy(v_hbm.at[0], v_s, sems.at[1])]
    copies += [pltpu.make_async_copy(w_hbm.at[m], w.at[m], sems.at[2 + m]) for m in range(3)]
    copies.append(pltpu.make_async_copy(r_hbm.at[0], r_s, sems.at[5]))
    for i in (0, 2, 3, 5, 1, 4):
        copies[i].start()
    me = me_ref[0]
    tok, width = k_s.shape

    def ready(name):
        for i in {"gate": (0, 2), "linear": (3,), "output": (5, 1, 4)}[name]:
            copies[i].wait()
        if name == "output":
            rate_col = jnp.broadcast_to(r_s[...], (8, tok)).T[:, :1]
            dy_s[...] = (rate_col * v_s[...].astype(f32)).astype(bf16)

    token_grads(k_s, dy_s, w, da_s, db_s, hid_s, 0, ready)
    over_tokens = ((0,), (0,))
    g_s[0] = dot(k_s[...], da_s[...], over_tokens).astype(bf16)
    g_s[1] = dot(k_s[...], db_s[...], over_tokens).astype(bf16)
    g_s[2] = dot(hid_s[...], dy_s[...], over_tokens).astype(bf16)
    rows = width // SHARDS // CHUNKS
    for h in range(CHUNKS):
        for out, relative in ((out_refs[2 * h], (1, 3, 5, 7)), (out_refs[2 * h + 1], (0, 2, 4, 6))):
            for i, r in enumerate(relative):
                place = pl.ds(pl.multiple_of(base_row(me ^ r, width) + h * rows, rows), rows)
                for m in range(3):
                    row = (3 * i + m) * rows
                    out[row : row + rows, :] = g_s[m, place, :]
        place = pl.ds(pl.multiple_of(base_row(me, width) + h * rows, rows), rows)
        for m in range(3):
            w0_refs[h][m * rows : (m + 1) * rows, :] = w[m, place, :]


def first_grads(me, k, v, r, init):
    _, tok, width = k.shape
    rows = 3 * width // 2 // CHUNKS
    square = pltpu.VMEM((tok, width), bf16)
    weights = pltpu.VMEM((3, width, width), bf16)
    return pl.pallas_call(
        first_grads_kernel,
        out_shape=[jax.ShapeDtypeStruct((rows, width), bf16)] * (2 * CHUNKS)
        + [jax.ShapeDtypeStruct((rows // 4, width), bf16)] * CHUNKS,
        in_specs=[SMEM] + [HBM] * 4,
        out_specs=[VMEM] * (3 * CHUNKS),
        scratch_shapes=[square, square, weights, square, square, square, square, weights, pltpu.VMEM((1, tok), f32), pltpu.SemaphoreType.DMA((6,))],
        compiler_params=params(),
        name="first_grads",
    )(me, in_hbm(k), in_hbm(v), in_hbm(r), in_hbm(init))


def next_grads_kernel(n_w, me_ref, own_hbm, other_hbm, *refs):
    w_refs, out_refs, w_out = refs[:n_w], refs[n_w : n_w + 4 * CHUNKS], refs[n_w + 4 * CHUNKS]
    tok_s, da_s, db_s, hid_s, g_s, w, sems = refs[n_w + 4 * CHUNKS + 1 :]
    loads = [
        [pltpu.make_async_copy(ref.at[j], tok_s.at[i, j], sems.at[2 * i + j]) for j in range(2)]
        for i, ref in enumerate((own_hbm, other_hbm))
    ]
    for pair in loads:
        for load in pair:
            load.start()
    me = me_ref[0]
    assemble(me, w_refs, w)
    keep_w = pltpu.make_async_copy(w, w_out, sems.at[4])
    tok, width = tok_s.shape[2:]
    half = width // 2
    for i, pair in enumerate(loads):

        def ready(name, pair=pair):
            if name != "linear":
                pair[name == "output"].wait()

        token_grads(tok_s.at[i, 0], tok_s.at[i, 1], w, da_s, db_s, hid_s, i * tok, ready)
    keep_w.start()
    mine = pl.ds(pl.multiple_of((me % 2) * half, half), half)
    over_tokens = ((0,), (0,))
    spans = ((0, slice(0, tok)), (1, slice(tok, 2 * tok)))
    for m, d_s in ((0, da_s), (1, db_s)):
        g_s[m] = sum(dot(tok_s[i, 0, :, mine], d_s[span, :], over_tokens) for i, span in spans).astype(bf16)
    g_s[2] = sum(dot(hid_s[span, mine], tok_s[i, 1], over_tokens) for i, span in spans).astype(bf16)
    rows = width // SHARDS // CHUNKS
    for h in range(CHUNKS):
        for i, r in enumerate((0, 2, 4, 6)):
            place = pl.ds(pl.multiple_of((me ^ r) // 2 * (rows * CHUNKS) + h * rows, rows), rows)
            for m in range(3):
                out_refs[4 * h + i][m * rows : (m + 1) * rows, :] = g_s[m, place, :]
    keep_w.wait()


def next_grads(me, own, other, w):
    _, tok, width = own.shape
    rows = 3 * width // SHARDS // CHUNKS
    return pl.pallas_call(
        functools.partial(next_grads_kernel, len(w)),
        out_shape=[jax.ShapeDtypeStruct((rows, width), bf16)] * (4 * CHUNKS) + [pltpu.HBM((3, width, width), bf16)],
        in_specs=[SMEM, HBM, HBM] + [VMEM] * len(w),
        out_specs=[VMEM] * (4 * CHUNKS) + [HBM],
        scratch_shapes=[pltpu.VMEM((2, 2, tok, width), bf16)]
        + [pltpu.VMEM((2 * tok, width), bf16)] * 3
        + [pltpu.VMEM((3, width // 2, width), bf16), pltpu.VMEM((3, width, width), bf16), pltpu.SemaphoreType.DMA((5,))],
        compiler_params=params(),
        name="next_grads",
    )(me, in_hbm(own), in_hbm(other), *w)


def tokens_kernel(k_hbm, v_hbm, r_hbm, out, k_s, v_s, r_s, sems):
    loads = [pltpu.make_async_copy(x.at[1], x_s, sems.at[i]) for i, (x, x_s) in enumerate(((v_hbm, v_s), (r_hbm, r_s), (k_hbm, k_s)))]
    for load in loads:
        load.start()
    tok = v_s.shape[0]
    loads[0].wait()
    loads[1].wait()
    rate_col = jnp.broadcast_to(r_s[...], (8, tok)).T[:, :1]
    v_s[...] = (rate_col * v_s[...].astype(f32)).astype(bf16)
    loads[2].wait()
    stores = [pltpu.make_async_copy(x_s, out.at[i], sems.at[3 + i]) for i, x_s in enumerate((k_s, v_s))]
    for store in stores:
        store.start()
    for store in stores:
        store.wait()


def next_tokens(k, v, r):
    _, tok, width = k.shape
    square = pltpu.VMEM((tok, width), bf16)
    return pl.pallas_call(
        tokens_kernel,
        out_shape=pltpu.HBM((2, tok, width), bf16),
        in_specs=[HBM] * 3,
        out_specs=HBM,
        scratch_shapes=[square, square, pltpu.VMEM((1, tok), f32), pltpu.SemaphoreType.DMA((5,))],
        compiler_params=params(),
        name="next_tokens",
    )(in_hbm(k), in_hbm(v), in_hbm(r))


def update_kernel(keep, p_ref, q_ref, w_ref, *refs):
    moment = p_ref[...].astype(f32) + q_ref[...].astype(f32)
    weights = w_ref[...].astype(f32)
    n_out = 3 if keep else 1
    if len(refs) > n_out:
        moment = momentum_beta * refs[0][...] + moment
    outs = refs[-n_out:]
    unit = moment * lax.rsqrt(jnp.mean(moment * moment, axis=-1, keepdims=True) + 1e-05)
    moved = weights + step_size * unit
    old_sq = jnp.mean(weights * weights, axis=-1, keepdims=True) + 1e-06
    new_sq = jnp.mean(moved * moved, axis=-1, keepdims=True) + 1e-06
    weights = moved * jnp.sqrt(old_sq / new_sq)
    outs[0][...] = weights.astype(bf16)
    if keep:
        outs[1][...] = weights
        outs[2][...] = moment


def update(p, q, state, keep):
    out = [jax.ShapeDtypeStruct(p.shape, bf16)] + [jax.ShapeDtypeStruct(p.shape, f32)] * (2 if keep else 0)
    got = pl.pallas_call(
        functools.partial(update_kernel, keep),
        out_shape=out,
        in_specs=[VMEM] * (2 + len(state)),
        out_specs=[VMEM] * len(out),
        compiler_params=params(),
        name="update",
    )(p, q, *state)
    return got[0], got[1:]


def apply_kernel(n_w, me_ref, q_ref, *refs):
    w_refs, out = refs[:n_w], refs[n_w]
    if n_w == 1:
        w = w_refs[0]
    else:
        w = refs[n_w + 1]
        assemble(me_ref[0], w_refs, w)
    tok = q_ref.shape[0]
    chunk = min(tok, 512)
    for t in range(0, tok, chunk):
        span = slice(t, t + chunk)
        q = q_ref[span, :]
        a = dot(q, w[0])
        b = dot(q, w[1])
        hid = (a * sigmoid(a) * b).astype(bf16)
        out[span, :] = dot(hid, w[2]).astype(bf16)


def fast_apply(me, q, block, w):
    _, tok, width = q.shape
    whole = pl.BlockSpec((3, width, width), lambda i: (0, 0, 0))
    return pl.pallas_call(
        functools.partial(apply_kernel, len(w)),
        grid=(1,),
        out_shape=jax.ShapeDtypeStruct((tok, width), bf16),
        in_specs=[SMEM, pl.BlockSpec((None, tok, width), lambda i: (block, 0, 0))] + ([whole] if len(w) == 1 else [VMEM] * len(w)),
        out_specs=VMEM,
        scratch_shapes=[pltpu.VMEM((3, width, width), bf16)] if len(w) > 1 else [],
        compiler_params=params(),
        name="apply",
    )(me, q, *w)


def project_own_kernel(o_ref, proj_ref, out):
    out[...] = dot(o_ref[...], proj_ref[...])


def project_own(o, proj):
    return pl.pallas_call(
        project_own_kernel,
        out_shape=jax.ShapeDtypeStruct((o.shape[0], proj.shape[1]), f32),
        in_specs=[VMEM] * 2,
        out_specs=VMEM,
        compiler_params=params(),
        name="project_own",
    )(o, proj)


def project_kernel(block, sum_ref, o_ref, proj_ref, *refs):
    out, (out_s, sems) = refs[-3], refs[-2:]
    rows = o_ref.shape[0] // 4
    stores = []
    for i in range(4):
        span = slice(i * rows, (i + 1) * rows)
        out_s[span, :] = (sum_ref[span, :] + dot(o_ref[span, :], proj_ref[...])).astype(bf16)
        stores.append(pltpu.make_async_copy(out_s.at[span, :], out.at[block, span, :], sems.at[i]))
        stores[-1].start()
    for store in stores:
        store.wait()


def project(block, blocks, own, o_other, proj_other, into):
    tok, cols = own.shape
    args = [own, o_other, proj_other] + ([] if into is None else [into])
    return pl.pallas_call(
        functools.partial(project_kernel, block),
        out_shape=jax.ShapeDtypeStruct((blocks, tok, cols), bf16),
        in_specs=[VMEM] * 3 + [pl.BlockSpec(memory_space=pl.ANY)] * (len(args) - 3),
        out_specs=pl.BlockSpec(memory_space=pl.ANY),
        scratch_shapes=[pltpu.VMEM((tok, cols), bf16), pltpu.SemaphoreType.DMA((4,))],
        input_output_aliases={} if into is None else {3: 0},
        compiler_params=params(),
        name="project",
    )(*args)


SHARDS = 8
CHUNKS = 2
FLOWS = ((1, 2), (2, 4), (3, 6))


def swap_low_bits(i):
    return (i & ~3) | ((i & 1) << 1) | ((i >> 1) & 1)


def together(*values):
    return lax.optimization_barrier(values)


def after(x, *others):
    return together(x, *others)[0]


def solution(mesh):
    ctx, heads = mesh.shape["ctx"], mesh.shape["head"]
    assert ctx & (ctx - 1) == 0 and ctx >= SHARDS and heads == 2

    def swap(x, bits):
        pairs = [(2 * i, 2 * (i ^ bits)) for i in range(ctx)]
        pairs += [(2 * i + 1, 2 * (i ^ swap_low_bits(bits)) + 1) for i in range(ctx)]
        return lax.ppermute(x, ("ctx", "head"), pairs)

    def swap_head(x):
        return lax.ppermute(x, "head", [(0, 1), (1, 0)])

    def add(x, y):
        return x.astype(f32) + y.astype(f32)

    def reduce_half(received, keep):
        total = add(keep, received)
        n = total.shape[0] // 4
        return [total[i * n : (i + 1) * n] for i in range(4)]

    def reduce_pieces(pieces, received):
        p = sum((x.astype(f32) for x in received), pieces[0].astype(f32)).astype(bf16)
        bit = SHARDS
        while bit < ctx // 2:
            p = add(p, swap(p, bit)).astype(bf16)
            bit *= 2
        return p

    def last_exchange(p):
        return swap(p, ctx // 2) if ctx > SHARDS else jnp.zeros_like(p)

    def on_device(queries, key_vectors, value_vectors, token_rates, fast_init, out_proj):
        blocks, tok, _, width = queries.shape
        assert blocks == 2
        flat = lambda x: x.reshape(blocks, tok, width)
        q, k, v = flat(queries), flat(key_vectors), flat(value_vectors)
        r = token_rates.reshape(blocks, 1, tok)
        init, proj_all = fast_init[0], out_proj[0]
        head = lax.axis_index("head")
        label = (lax.axis_index("ctx") % SHARDS).astype(jnp.int32)
        me = jnp.where(head == 0, label, swap_low_bits(label)).reshape(1)
        half = proj_all.shape[1] // heads
        proj = lax.dynamic_slice_in_dim(proj_all, head * half, half, 1)
        proj_other = swap_head(lax.dynamic_slice_in_dim(proj_all, (1 - head) * half, half, 1))

        def finish(c, me, w, into):
            o = fast_apply(me, q, c, w)
            return project(c, blocks, project_own(o, proj), swap_head(o), proj_other, into)

        result = None
        for c in range(blocks):
            last = c + 1 == blocks
            if c == 0:
                grads = first_grads(me, k, v, r, init)
                state = [[w0] for w0 in grads[2 * CHUNKS :]]
                tokens = next_tokens(*together(k, v, r, grads[0])[:3])
                received = [swap(grads[2 * h], 1) for h in range(CHUNKS)]
                pieces = [reduce_half(received[h], grads[2 * h + 1]) for h in range(CHUNKS)]
            else:
                grads = next_grads(me, tokens, tokens_other, w)
                pieces = [grads[4 * h : 4 * h + 4] for h in range(CHUNKS)]
            received = {h: [swap(pieces[h][i].astype(bf16), bits) for i, bits in FLOWS] for h in range(CHUNKS)[:: -1 if last else 1]}
            sums = [reduce_pieces(pieces[h], received[h]) for h in range(CHUNKS)]
            others = [last_exchange(p) for p in sums]
            near = []
            for h in range(CHUNKS):
                if h:
                    others[h] = after(others[h], near[-1][0])
                wb, state[h] = update(sums[h], others[h], state[h], not last)
                got = {bits: swap(wb, bits) for _, bits in FLOWS}
                near.append([wb] + [got[bits] for bits in (2, 4, 6)])
                if not last and h == 0:
                    tokens_other = swap(after(tokens, sums[0]), 1)
            joined, far = [], []
            for h in range(CHUNKS):
                parts = list(near[h])
                if h and last:
                    parts[0] = after(parts[0], joined[-1])
                joined.append(jnp.concatenate(parts))
                far.append(swap(joined[-1], 1))
            if c > 0:
                me_late = after(me, near[1][0])
                result = finish(c - 1, me_late, grads[4 * CHUNKS :], result)
                me, result = together(me, result)
            w = [x for h in range(CHUNKS) for x in (*near[h], far[h])]
        return finish(blocks - 1, me, w, result)

    placed = (
        P(None, "ctx", "head", None),
        P(None, "ctx", "head", None),
        P(None, "ctx", "head", None),
        P(None, "ctx", "head"),
        P("head", None, None, None),
        P("head", None, None),
    )
    return jax.shard_map(on_device, mesh=mesh, in_specs=placed, out_specs=P(None, "ctx", "head"), check_vma=False)
```
